256 devices in a mesh: wide: 32 (over x, z), narrow: 8 (over y, core).
Axes of the slice: x: 4, y: 4, z: 8, core: 2. Of those that a mesh axis runs over, the one named last changes fastest.
Arguments:
- latent: bfloat16 [8192, 4096], P('wide', 'narrow'), may hold values from -90 to 90
- actions: int32 [8192], P('wide'), may hold values from 0 to 255
- action_table: bfloat16 [256, 4096], P(None, 'narrow'), may hold values from -3 to 3
- norm1_gain: float32 [4096], P('narrow'), may hold values from 0.5 to 1.5
- w_query: bfloat16 [4096, 2048], P(None, 'narrow'), may hold values from -0.140625 to 0.140625
- w_key: bfloat16 [4096, 2048], P(None, 'narrow'), may hold values from -0.140625 to 0.140625
- w_value: bfloat16 [4096, 2048], P(None, 'narrow'), may hold values from -0.09375 to 0.09375
- w_out: bfloat16 [2048, 4096], P(None, 'narrow'), may hold values from -0.125 to 0.125
- key_cache: bfloat16 [64, 512, 2048], P('wide', None, 'narrow'), may hold values from -460 to 460
- value_cache: bfloat16 [64, 512, 2048], P('wide', None, 'narrow'), may hold values from -6 to 6
- norm2_gain: float32 [4096], P('narrow'), may hold values from 0.5 to 1.5
- policy_in: bfloat16 [4096, 512], P('narrow'), may hold values from -0.09375 to 0.09375
- value_in: bfloat16 [4096, 512], P('narrow'), may hold values from -0.09375 to 0.09375
- policy_out: bfloat16 [512, 256], replicated, may hold values from -12.5 to 12.5
- value_out: bfloat16 [512], replicated, may hold values from -0.25 to 0.25
- targets: int32 [8192], P('wide'), may hold values from 0 to 255
- returns: float32 [8192], P('wide'), may hold values from -19 to 19
Outputs:
- new_latent: bfloat16 [8192, 4096], P('wide', 'narrow')
- losses: float32 [2], replicated
- policy_in_grad: bfloat16 [4096, 512], P('narrow')
- value_in_grad: bfloat16 [4096, 512], P('narrow')
- policy_out_grad: bfloat16 [512, 256], replicated
- value_out_grad: bfloat16 [512], replicated
The draws below stay inside these ranges and needn't reach their ends.
All inputs are finite; a program needn't handle non-finite values.
Results may differ from the reference program's by a relative error of at most 0.019.
Values may be sent and summed in bfloat16 or wider, within the bound.
A program may use at most 64 MiB of HBM per device.

```python
import math
import jax
import jax.numpy as jnp
from jax import lax

D = 4096
HEADS = 16
HD = 128
CTX = 512
BRANCH = 128
PH = 512
VH = 512
A = 256
HF = 2048
SCENES = 64
ROWS = 8192


def shared_projection(key):
    return jnp.clip(jax.random.normal(key, (D, HF), jnp.float32), -6.0, 6.0) * D ** (-0.5)


def draw_w_query(key, part):
    shared = shared_projection(key)
    key = jax.random.fold_in(key, 15)
    extra = jnp.clip(jax.random.normal(key, (D, HF), jnp.float32), -6.0, 6.0) * D ** (-0.5)
    return (0.8 * shared + 0.6 * extra).astype(jnp.bfloat16)


def draw_w_key(key, part):
    shared = shared_projection(key)
    key = jax.random.fold_in(key, 16)
    extra = jnp.clip(jax.random.normal(key, (D, HF), jnp.float32), -6.0, 6.0) * D ** (-0.5)
    return (0.6 * shared + 0.8 * extra).astype(jnp.bfloat16)


def draw_latent(key, part):
    key = jax.random.fold_in(key, 11)
    key_a, key_b, key_c = jax.random.split(key, 3)
    row_scale = jnp.exp(jax.random.uniform(key_a, (ROWS, 1), jnp.float32, math.log(0.3), math.log(3.0)))
    col_pos = jnp.arange(D).astype(jnp.float32) / D
    col_scale = jnp.exp(math.log(10.0) * (col_pos - 0.5))[None, :] * jnp.exp(jax.random.uniform(key_b, (1, D), jnp.float32, -0.35, 0.35))
    base = jnp.clip(jax.random.normal(key_c, (ROWS, D), jnp.float32), -6.0, 6.0)
    return (base * row_scale * col_scale).astype(jnp.bfloat16)


def draw_key_cache(key, part):
    key = jax.random.fold_in(key, 12)
    key_a = jax.random.fold_in(key, 0)
    base = jnp.clip(jax.random.normal(key_a, (SCENES, CTX, HF), jnp.float32), -6.0, 6.0)
    return base.astype(jnp.bfloat16)


def draw_policy_out(key, part):
    key = jax.random.fold_in(key, 13)
    key_a = jax.random.fold_in(key, 0)
    base = 0.3 * jnp.clip(jax.random.normal(key_a, (PH, A), jnp.float32), -6.0, 6.0)
    return base.astype(jnp.bfloat16)


def draw_returns(key, part):
    key = jax.random.fold_in(key, 14)
    rising = jnp.exp(math.log(3.0) * jnp.arange(ROWS).astype(jnp.float32) / ROWS)
    base = jnp.clip(jax.random.normal(key, (ROWS,), jnp.float32), -6.0, 6.0)
    return base * rising


def with_ends(drawn, stream_key, smallest, high):
    longest = drawn.shape.index(max(drawn.shape))
    spots = []
    for shift in (0, 1):
        where = [jax.random.randint(jax.random.fold_in(stream_key, axis), (), 0, length) for axis, length in enumerate(drawn.shape)]
        where[longest] = (where[longest] + shift) % drawn.shape[longest]
        spots.append(tuple(where))
    return drawn.at[spots[0]].set(smallest).at[spots[1]].set(high)


def levels(rng, shape, pieces, low, high):
    def one(dim, blocks):
        steps = jax.random.uniform(jax.random.fold_in(jax.random.fold_in(rng, 6), dim), (blocks,), jnp.float32, low / len(pieces), high / len(pieces))
        return jnp.repeat(jnp.exp(steps), shape[dim] // blocks).reshape((-1,) + (1,) * (len(shape) - dim - 1))

    level = one(*pieces[0])
    for cut in pieces[1:]:
        level = level * one(*cut)
    return level


def normal_values(own_key, dims, width, bound, shards=(), kind=jnp.bfloat16):
    level = levels(own_key, dims, shards, -0.22, 0.18) if shards else 1.0
    values = jax.random.normal(own_key, dims, jnp.float32) * width * level
    return jnp.minimum(jnp.maximum(values, -bound), bound).astype(kind)


def setup_inputs(seed: int = 0) -> dict:
    keys = jax.random.split(jax.random.key(seed), 18)
    return {
        "latent": draw_latent(jax.random.fold_in(keys[17], 71), 0),
        "actions": with_ends(jax.random.randint(keys[1], (ROWS,), 0, A), jax.random.fold_in(keys[1], 1), 0, A - 1).astype(jnp.int32),
        "action_table": normal_values(keys[2], (A, D), 0.5, 3.0, ((1, 8),)),
        "norm1_gain": jnp.clip(1.0 + 0.1 * jax.random.normal(keys[3], (D,), jnp.float32), 0.5, 1.5),
        "w_query": draw_w_query(jax.random.fold_in(keys[17], 71), 0),
        "w_key": draw_w_key(jax.random.fold_in(keys[17], 71), 0),
        "w_value": normal_values(keys[6], (D, HF), D ** -0.5, 0.09375, ((1, 8),)),
        "w_out": normal_values(keys[7], (HF, D), HF ** -0.5, 0.125, ((1, 8),)),
        "key_cache": draw_key_cache(jax.random.fold_in(keys[17], 71), 0),
        "value_cache": normal_values(keys[9], (SCENES, CTX, HF), 1.0, 6.0, ((0, 32), (2, 8))),
        "norm2_gain": jnp.clip(1.0 + 0.1 * jax.random.normal(keys[10], (D,), jnp.float32), 0.5, 1.5),
        "policy_in": normal_values(keys[11], (D, PH), D ** -0.5, 0.09375, ((0, 8),)),
        "value_in": normal_values(keys[12], (D, VH), D ** -0.5, 0.09375, ((0, 8),)),
        "policy_out": draw_policy_out(jax.random.fold_in(keys[17], 71), 0),
        "value_out": normal_values(keys[14], (VH,), VH ** -0.5, 0.25),
        "targets": with_ends(jax.random.randint(keys[15], (ROWS,), 0, A), jax.random.fold_in(keys[15], 1), 0, A - 1).astype(jnp.int32),
        "returns": draw_returns(jax.random.fold_in(keys[17], 71), 0),
    }


EPSILON = 1e-05

def silu_slope(values):
    sigma = jax.nn.sigmoid(values)
    return sigma * (1.0 + values * (1.0 - sigma))

def reference(latent, actions, action_table, norm1_gain, w_query, w_key, w_value, w_out, key_cache, value_cache, norm2_gain, policy_in, value_in, policy_out, value_out, targets, returns):
    tokens = latent.astype(jnp.float32) + action_table.astype(jnp.float32)[actions]
    inverse = lax.rsqrt(lax.optimization_barrier(jnp.mean(tokens * tokens, axis=1, keepdims=True)) + EPSILON)
    normed = (tokens * inverse * norm1_gain).astype(jnp.bfloat16)
    query = jnp.dot(normed, w_query, preferred_element_type=jnp.float32).astype(jnp.bfloat16)
    key_new = jnp.dot(normed, w_key, preferred_element_type=jnp.float32).astype(jnp.bfloat16)
    value_new = jnp.dot(normed, w_value, preferred_element_type=jnp.float32).astype(jnp.bfloat16)
    scaling = HD ** (-0.5)

    def one_scene(packed):
        query_s, keyn_s, valuen_s, kcache_s, vcache_s = packed
        query_f = query_s.astype(jnp.float32)
        scores = jnp.einsum('bhd,chd->bhc', query_f, kcache_s.astype(jnp.float32), precision=lax.Precision.HIGHEST) * scaling
        own_score = lax.optimization_barrier(jnp.sum(query_f * keyn_s.astype(jnp.float32), axis=-1)) * scaling
        highest = jnp.maximum(lax.optimization_barrier(jnp.max(scores, axis=-1)), own_score)
        expd = jnp.exp(scores - highest[..., None])
        own_exp = jnp.exp(own_score - highest)
        totals = lax.optimization_barrier(jnp.sum(expd, axis=-1)) + own_exp
        weights = (expd / totals[..., None]).astype(jnp.bfloat16)
        own_weight = (own_exp / totals).astype(jnp.bfloat16)
        mixed = jnp.einsum('bhc,chd->bhd', weights.astype(jnp.float32), vcache_s.astype(jnp.float32), precision=lax.Precision.HIGHEST)
        mixed = mixed + own_weight.astype(jnp.float32)[..., None] * valuen_s.astype(jnp.float32)
        return mixed.astype(jnp.bfloat16)
    packed = (query.reshape(SCENES, BRANCH, HEADS, HD), key_new.reshape(SCENES, BRANCH, HEADS, HD), value_new.reshape(SCENES, BRANCH, HEADS, HD), key_cache.reshape(SCENES, CTX, HEADS, HD), value_cache.reshape(SCENES, CTX, HEADS, HD))
    attended = lax.map(one_scene, packed).reshape(ROWS, HF)
    state = tokens + jnp.dot(attended, w_out, preferred_element_type=jnp.float32)
    new_latent = state.astype(jnp.bfloat16)
    inverse_two = lax.rsqrt(lax.optimization_barrier(jnp.mean(state * state, axis=1, keepdims=True)) + EPSILON)
    heads_in = (state * inverse_two * norm2_gain).astype(jnp.bfloat16)
    policy_pre = jnp.dot(heads_in, policy_in, preferred_element_type=jnp.float32)
    value_pre = jnp.dot(heads_in, value_in, preferred_element_type=jnp.float32)
    policy_hidden = jax.nn.silu(policy_pre).astype(jnp.bfloat16)
    value_hidden = jax.nn.silu(value_pre).astype(jnp.bfloat16)
    logits = jnp.dot(policy_hidden, policy_out, preferred_element_type=jnp.float32)
    value = jnp.dot(value_hidden, value_out, preferred_element_type=jnp.float32)
    highest = lax.optimization_barrier(jnp.max(logits, axis=1, keepdims=True))
    log_total = highest[:, 0] + jnp.log(lax.optimization_barrier(jnp.sum(jnp.exp(logits - highest), axis=1)))
    onehot = (targets[:, None] == jnp.arange(A, dtype=jnp.int32)[None, :]).astype(jnp.float32)
    picked = lax.optimization_barrier(jnp.sum(logits * onehot, axis=1))
    errors = value - returns
    losses = jnp.stack([jnp.mean(log_total - picked), 0.5 * jnp.mean(errors * errors)])
    factor = ROWS ** (-0.5)
    dlogits = ((jnp.exp(logits - log_total[:, None]) - onehot) * factor).astype(jnp.bfloat16)
    dvalue = (errors * factor).astype(jnp.bfloat16)
    policy_out_grad = jnp.dot(policy_hidden.T, dlogits, preferred_element_type=jnp.float32).astype(jnp.bfloat16)
    value_out_grad = jnp.dot(dvalue, value_hidden, preferred_element_type=jnp.float32).astype(jnp.bfloat16)
    policy_dpre = (jnp.dot(dlogits, policy_out.T, preferred_element_type=jnp.float32) * silu_slope(policy_pre)).astype(jnp.bfloat16)
    value_dpre = (dvalue.astype(jnp.float32)[:, None] * value_out.astype(jnp.float32)[None, :] * silu_slope(value_pre)).astype(jnp.bfloat16)
    policy_in_grad = jnp.dot(heads_in.T, policy_dpre, preferred_element_type=jnp.float32).astype(jnp.bfloat16)
    value_in_grad = jnp.dot(heads_in.T, value_dpre, preferred_element_type=jnp.float32).astype(jnp.bfloat16)
    return (new_latent, losses, policy_in_grad, value_in_grad, policy_out_grad, value_out_grad)
```

```python
import functools

import jax
import jax.numpy as jnp
from jax import lax
from jax.experimental import pallas as pl
from jax.experimental.pallas import tpu as pltpu
from jax.sharding import PartitionSpec as P

HD = 128
EPSILON = 1e-05
X, Y, Z = 4, 4, 8
NARROW = 2 * Y
MESH = pl.DeviceIdType.MESH
F32, BF16 = jnp.float32, jnp.bfloat16
COPIES = 200


def nt_dot(left, right):
    return lax.dot_general(left, right, (((1,), (1,)), ((), ())), preferred_element_type=F32)


def dot(left, right):
    return jnp.dot(left, right, preferred_element_type=F32)


def kernel(
    latent_in,
    actions_in,
    table_in,
    gain1_in,
    w_query_in,
    w_key_in,
    w_value_in,
    w_out_in,
    keys_in,
    values_in,
    gain2_in,
    policy_in_in,
    value_in_in,
    policy_out_in,
    value_out_in,
    targets_in,
    returns_in,
    latent_out,
    grads_out,
    policy_out_grad,
    misc_out,
    latent,
    actions,
    table,
    gain1,
    w_qkv,
    w_out,
    keys,
    values,
    gain2,
    heads_w,
    policy_out,
    value_out,
    targets,
    returns,
    normed,
    squares,
    tokens,
    qkv,
    attended,
    gained_t,
    pre_send,
    pre_recv,
    onehot,
    returns_col,
    dpre_send,
    dpre_recv,
    factor_send,
    factor_recv,
    misc_send,
    misc_recv,
    grad_f32,
    grad_send,
    grad_recv,
    block_f32,
    block_send,
    block_recv,
    block_mid,
    block_recv_z,
    misc_x,
    misc_z,
    load_sem,
    send_sem,
    recv_sem,
):
    wide, narrow = lax.axis_index("wide"), lax.axis_index("narrow")
    x, z = wide // Z, lax.rem(wide, Z)
    y, c = narrow // 2, lax.rem(narrow, 2)
    scenes, branch, width = normed.shape[1:]
    total_rows = scenes * branch * X * Z
    full_width = width * NARROW

    def device(dx=0, dy=0, dz=0, dc=0):
        return (
            lax.rem(x + dx, X) * Z + lax.rem(z + dz, Z),
            lax.rem(y + dy, Y) * 2 + lax.rem(c + dc, 2),
        )

    plane = [(dx, dy, dc) for dx in (2, 1, 3, 0) for dy in (2, 1, 3, 0) for dc in (1, 0)]
    plane = [o for o in plane if o != (0, 0, 0)]
    z_steps = (4, 3, 5, 2, 6, 1, 7)
    x_steps = (2, 1, 3)
    y_steps = (2, 1, 3)
    barrier = pltpu.get_barrier_semaphore()
    partners = [device(dx, dy, 0, dc) for dx, dy, dc in plane] + [device(dz=d) for d in z_steps]
    for partner in partners:
        pl.semaphore_signal(barrier, inc=1, device_id=partner, device_id_type=MESH)

    loads = {}

    def load(name, source, target):
        copy = pltpu.make_async_copy(source, target, load_sem.at[len(loads)])
        copy.start()
        loads[name] = copy

    load("actions", actions_in, actions)
    load("table", table_in, table)
    load("latent", latent_in, latent)
    load("gain1", gain1_in, gain1)
    load("w_query", w_query_in, w_qkv.at[0])
    load("w_key", w_key_in, w_qkv.at[1])
    load("w_value", w_value_in, w_qkv.at[2])
    load("keys", keys_in, keys)
    load("values", values_in, values)
    load("w_out", w_out_in, w_out)
    load("gain2", gain2_in, gain2)
    load("policy_in", policy_in_in, heads_w.at[0])
    load("value_in", value_in_in, heads_w.at[1])
    load("policy_out", policy_out_in, policy_out)
    load("value_out", value_out_in, value_out)
    load("targets", targets_in, targets)
    load("returns", returns_in, returns)

    started = []

    def send(source, target, partner):
        i = len(started)
        copy = pltpu.make_async_remote_copy(
            src_ref=source,
            dst_ref=target,
            send_sem=send_sem.at[i],
            recv_sem=recv_sem.at[i],
            device_id=partner,
            device_id_type=MESH,
        )
        copy.start()
        started.append(copy)
        return copy

    for name in ("actions", "table", "latent", "gain1"):
        loads[name].wait()
    action_count = table.shape[0]
    action_ids = lax.broadcasted_iota(jnp.int32, (action_count, branch), 0)
    for s in range(scenes):
        chosen = (actions[s : s + 1, :] == action_ids).astype(F32).T.astype(BF16)
        token = latent[s].astype(F32) + dot(chosen, table[...])
        tokens[s] = token
        normed[narrow, s] = (token * gain1[...]).astype(BF16)
        square = token * token
        square = sum(square[:, i : i + 128] for i in range(0, width, 128))
        squares[narrow, s : s + 1, :] = jnp.sum(square.T, axis=0, keepdims=True)

    pl.semaphore_wait(barrier, len(partners))

    def gather_start(buffer, s):
        own = buffer.at[narrow, s]
        near = send(own, own, device(dc=1))
        far = [send(own, own, device(dy=d)) for d in y_steps]
        return near, far

    def gather_slots(buffer, s, near, far):
        yield narrow
        near.wait_recv()
        yield y * 2 + 1 - c
        passed = []
        for d, copy in zip(y_steps, far):
            slot = lax.rem(y - d + Y, Y) * 2 + c
            copy.wait_recv()
            passed.append(send(buffer.at[slot, s], buffer.at[slot, s], device(dc=1)))
            yield slot
        for d, copy in zip(y_steps, passed):
            copy.wait_recv()
            yield lax.rem(y - d + Y, Y) * 2 + 1 - c

    gathers = [gather_start(normed, 0)]
    square_copies = [
        send(squares.at[narrow], squares.at[narrow], device(dy=dy, dc=dc))
        for dx, dy, dc in plane
        if dx == 0
    ]
    gathers.append(gather_start(normed, 1))

    loads["targets"].wait()
    loads["returns"].wait()
    for s in range(scenes):
        onehot[s] = (targets[s : s + 1, :] == action_ids).astype(F32).T
        returns_col[s] = jnp.broadcast_to(returns[s : s + 1, :], (128, branch)).T

    for name in ("w_query", "w_key", "w_value", "keys", "values"):
        loads[name].wait()
    scaling = HD ** (-0.5)
    heads_local = w_qkv.shape[2] // HD
    attended_copies = []
    for s in range(scenes):
        first = True
        for slot in gather_slots(normed, s, *gathers[s]):
            rows = normed[slot, s]
            for i in range(3):
                product = dot(rows, w_qkv[i, pl.ds(pl.multiple_of(slot * width, width), width), :])
                if first:
                    qkv[i] = product
                else:
                    qkv[i] += product
            first = False
        if s == 0:
            for copy in square_copies:
                copy.wait_recv()
        total = jnp.sum(squares[:, s : s + 1, :], axis=0)
        inverse = lax.rsqrt(total / full_width + EPSILON)
        inverse = jnp.broadcast_to(inverse, (128, branch)).T
        for h in range(heads_local):
            cols = slice(h * HD, (h + 1) * HD)
            query, key_new, value_new = ((qkv[i, :, cols] * inverse).astype(BF16) for i in range(3))
            scores = nt_dot(query, keys[s, :, cols]) * scaling
            own_score = (
                jnp.sum(query.astype(F32) * key_new.astype(F32), axis=1, keepdims=True) * scaling
            )
            highest = jnp.maximum(jnp.max(scores, axis=1, keepdims=True), own_score)
            expd = jnp.exp(scores - highest)
            own_exp = jnp.exp(own_score - highest)
            share = 1.0 / (jnp.sum(expd, axis=1, keepdims=True) + own_exp)
            weights = (expd * share).astype(BF16)
            own_weight = (own_exp * share).astype(BF16).astype(F32)
            mixed = dot(weights, values[s, :, cols]) + own_weight * value_new.astype(F32)
            attended[narrow, s, :, cols] = mixed.astype(BF16)
        attended_copies.append(gather_start(attended, s))

    for name in ("w_out", "gain2", "policy_in", "value_in"):
        loads[name].wait()
    heads_width = heads_w.shape[2]
    both = 2 * heads_width
    depth = attended.shape[3]
    share_rows = branch // NARROW
    my_rows = pl.ds(pl.multiple_of(narrow * share_rows, share_rows), share_rows)
    pre_copies, state_copies = [], []
    for s in range(scenes):
        for slot in gather_slots(attended, s, *attended_copies[s]):
            tokens[s] += dot(
                attended[slot, s], w_out[pl.ds(pl.multiple_of(slot * depth, depth), depth), :]
            )
        state = tokens[s]
        gained = state * gain2[...]
        gained_b = gained.astype(BF16)
        for i in range(2):
            pre_send[s, :, i * heads_width : (i + 1) * heads_width] = dot(
                gained_b, heads_w[i]
            ).astype(BF16)
        square = jnp.sum(state * state, axis=1, keepdims=True)
        high = square.astype(BF16)
        low = (square - high.astype(F32)).astype(BF16)
        lane = lax.broadcasted_iota(jnp.int32, (branch, 128), 1)
        pre_send[s, :, both:] = jnp.where(lane < 64, high.astype(F32), low.astype(F32)).astype(BF16)
        copies = []
        for dx, dy, dc in plane:
            if dx == 0:
                partner = device(dy=dy, dc=dc)
                rows = pl.ds(pl.multiple_of(partner[1] * share_rows, share_rows), share_rows)
                copies.append(send(pre_send.at[s, rows], pre_recv.at[narrow, s], partner))
        pre_copies.append(copies)
        pre_recv[narrow, s] = pre_send[s, my_rows, :]
        latent_out[s] = state.astype(BF16)
        gained_t[x, s] = gained.T.astype(BF16)
        state_copies.append(
            [send(gained_t.at[x, s], gained_t.at[x, s], device(dx=d)) for d in x_steps]
        )

    loads["policy_out"].wait()
    loads["value_out"].wait()
    for copies in pre_copies:
        for copy in copies:
            copy.wait_recv()
    sums = jnp.concatenate(
        [sum(pre_recv[i, s].astype(F32) for i in range(NARROW)) for s in range(scenes)], axis=0
    )
    square = sums[:, both : both + 1] + sums[:, both + 64 : both + 65]
    inverse = lax.rsqrt(square / full_width + EPSILON)
    pre = sums[:, :both] * inverse
    sigma = 1.0 / (1.0 + jnp.exp(-pre))
    hidden = (pre * sigma).astype(BF16)
    slope = sigma * (1.0 + pre * (1.0 - sigma))
    policy_hidden, value_hidden = hidden[:, :heads_width], hidden[:, heads_width:].astype(F32)
    logits = dot(policy_hidden, policy_out[...])
    value = jnp.sum(value_hidden * value_out[...], axis=1, keepdims=True)
    top = jnp.max(logits, axis=1, keepdims=True)
    log_total = top + jnp.log(jnp.sum(jnp.exp(logits - top), axis=1, keepdims=True))
    target = jnp.concatenate([onehot[s, my_rows, :] for s in range(scenes)], axis=0)
    wanted = jnp.concatenate([returns_col[s, my_rows, :] for s in range(scenes)], axis=0)
    picked = jnp.sum(logits * target, axis=1, keepdims=True)
    errors = value - wanted[:, 0:1]
    factor = total_rows ** (-0.5)
    dlogits = ((jnp.exp(logits - log_total) - target) * factor).astype(BF16)
    dvalue = (errors * factor).astype(BF16).astype(F32)
    dhidden = nt_dot(dlogits, policy_out[...])
    dpre_policy = (dhidden * slope[:, :heads_width] * inverse).astype(BF16)
    dpre_value = (dvalue * value_out[...] * slope[:, heads_width:] * inverse).astype(BF16)
    dpre = jnp.concatenate([dpre_policy, dpre_value], axis=1)
    cols = both // X
    for i in range(X):
        for s in range(scenes):
            dpre_send[i, s] = dpre[s * share_rows : (s + 1) * share_rows, i * cols : (i + 1) * cols]
    dpre_recv[x, :, my_rows, :] = dpre_send[x]
    dpre_copies = []
    for dx, dy, dc in plane:
        dpre_copies.append(
            send(
                dpre_send.at[lax.rem(x + dx, X)],
                dpre_recv.at[x, :, my_rows, :],
                device(dx=dx, dy=dy, dc=dc),
            )
        )

    block = heads_width // Y
    lanes = lax.broadcasted_iota(jnp.int32, (1, 128), 1)
    sum_policy = jnp.sum(log_total - picked, axis=0, keepdims=True)
    sum_value = 0.5 * jnp.sum(errors * errors, axis=0, keepdims=True)
    loss_row = jnp.where(lanes == 0, sum_policy, jnp.where(lanes == 1, sum_value, 0.0))
    value_row = jnp.sum(dvalue * value_hidden, axis=0, keepdims=True)
    for i in range(Y):
        for j in range(2):
            factor_send[2 * i + j, :, :block] = policy_hidden[:, i * block : (i + 1) * block]
            factor_send[2 * i + j, :, block:] = dlogits[:, j * 128 : (j + 1) * 128]
        misc_send[i] = jnp.concatenate(
            [value_row[:, i * block : (i + 1) * block], loss_row, jnp.zeros((6, 128), F32)], axis=0
        )
    factor_recv[narrow] = factor_send[narrow]
    misc_recv[narrow] = misc_send[y]
    factor_copies = []
    for dx, dy, dc in plane:
        if dx == 0:
            partner = device(dy=dy, dc=dc)
            factor_copies.append(send(factor_send.at[partner[1]], factor_recv.at[narrow], partner))
            factor_copies.append(
                send(misc_send.at[lax.rem(y + dy, Y)], misc_recv.at[narrow], partner)
            )

    for copies in state_copies:
        for copy in copies:
            copy.wait_recv()
    for copy in dpre_copies:
        copy.wait_recv()
    grad = None
    for i in range(X):
        for s in range(scenes):
            product = dot(gained_t[i, s], dpre_recv[i, s])
            grad = product if grad is None else grad + product
    grad_f32[...] = grad
    grad_send[...] = grad.astype(BF16)
    grad_rows = width // Z
    grad_copies = []
    for d in z_steps:
        rows = pl.ds(pl.multiple_of(lax.rem(z + d, Z) * grad_rows, grad_rows), grad_rows)
        grad_copies.append(send(grad_send.at[rows], grad_recv.at[d - 1], device(dz=d)))

    for copy in factor_copies:
        copy.wait_recv()
    left = jnp.concatenate([factor_recv[i, :, :block] for i in range(NARROW)], axis=0)
    right = jnp.concatenate([factor_recv[i, :, block:] for i in range(NARROW)], axis=0)
    part = dot(left.astype(F32).T.astype(BF16), right)
    block_f32[...] = part
    block_send[...] = part.astype(BF16)
    misc_x[0] = sum(misc_recv[i] for i in range(NARROW))
    block_rows = block // X
    block_copies = []
    for d in x_steps:
        rows = pl.ds(pl.multiple_of(lax.rem(x + d, X) * block_rows, block_rows), block_rows)
        block_copies.append(send(block_send.at[rows], block_recv.at[d - 1], device(dx=d)))
        block_copies.append(send(misc_x.at[0], misc_x.at[d], device(dx=d)))

    for copy in grad_copies:
        copy.wait_recv()
    my_grad = pl.ds(pl.multiple_of(z * grad_rows, grad_rows), grad_rows)
    my_cols = pl.ds(pl.multiple_of(lax.rem(x, 2) * cols, cols), cols)
    reduced = grad_f32[my_grad, :] + sum(grad_recv[i].astype(F32) for i in range(Z - 1))
    grads_out[x // 2, my_grad, my_cols] = reduced.astype(BF16)

    def spread(rows, **step):
        place = grads_out.at[x // 2, rows, my_cols]
        return send(place, place, device(**step))

    along_z = [spread(my_grad, dz=d) for d in z_steps]
    along_x = [spread(my_grad, dx=d) for d in x_steps]

    for copy in block_copies:
        copy.wait_recv()
    my_block = pl.ds(pl.multiple_of(x * block_rows, block_rows), block_rows)
    reduced = block_f32[my_block, :] + sum(block_recv[i].astype(F32) for i in range(X - 1))
    block_mid[...] = reduced.astype(BF16)
    misc_z[0] = sum(misc_x[i] for i in range(X))
    block_copies = []
    for d in z_steps:
        block_copies.append(send(block_mid, block_recv_z.at[d - 1], device(dz=d)))
        block_copies.append(send(misc_z.at[0], misc_z.at[d], device(dz=d)))

    def forward(d, copy):
        copy.wait_recv()
        rows = pl.ds(pl.multiple_of(lax.rem(z - d + Z, Z) * grad_rows, grad_rows), grad_rows)
        along_x.extend(spread(rows, dx=e) for e in x_steps)

    for d, copy in list(zip(z_steps, along_z))[::-1][:5]:
        forward(d, copy)

    for copy in block_copies:
        copy.wait_recv()
    reduced = reduced + sum(block_recv_z[i].astype(F32) for i in range(Z - 1))
    block_cols = pl.ds(pl.multiple_of(c * 128, 128), 128)
    place = policy_out_grad.at[
        pl.ds(pl.multiple_of(y * block + x * block_rows, block_rows), block_rows), block_cols
    ]
    place[...] = reduced.astype(BF16)
    block_copies = [send(place, place, device(dx=d)) for d in x_steps]
    misc_out[y] = sum(misc_z[i] for i in range(Z))
    misc_copies = [send(misc_out.at[y], misc_out.at[y], device(dy=d)) for d in y_steps]

    for d, copy in list(zip(z_steps, along_z))[::-1][5:]:
        forward(d, copy)

    for copy in block_copies:
        copy.wait_recv()
    place = policy_out_grad.at[pl.ds(pl.multiple_of(y * block, block), block), block_cols]
    block_copies = [send(place, place, device(dy=dy, dc=dc)) for dx, dy, dc in plane if dx == 0]

    for copy in misc_copies + along_x + block_copies:
        copy.wait_recv()
    for copy in started:
        copy.wait_send()


def per_device(
    latent,
    actions,
    action_table,
    norm1_gain,
    w_query,
    w_key,
    w_value,
    w_out,
    key_cache,
    value_cache,
    norm2_gain,
    policy_in,
    value_in,
    policy_out,
    value_out,
    targets,
    returns,
):
    rows, width = latent.shape
    scenes = key_cache.shape[0]
    branch = rows // scenes
    heads_width = policy_in.shape[1]
    features = w_query.shape[1]
    share = branch // NARROW
    block = heads_width // Y
    cols = 2 * heads_width // X
    total_rows = rows * X * Z
    vmem = pltpu.VMEM
    operands = (
        latent.reshape(scenes, branch, width),
        actions.reshape(scenes, branch),
        action_table,
        norm1_gain.reshape(1, width),
        w_query,
        w_key,
        w_value,
        w_out,
        key_cache,
        value_cache,
        norm2_gain.reshape(1, width),
        policy_in,
        value_in,
        policy_out,
        value_out.astype(F32).reshape(1, heads_width),
        targets.reshape(scenes, branch),
        returns.reshape(scenes, branch),
    )
    scratch = [
        vmem((scenes, branch, width), BF16),
        vmem((scenes, branch), jnp.int32),
        vmem(action_table.shape, BF16),
        vmem((1, width), F32),
        vmem((3,) + w_query.shape, BF16),
        vmem(w_out.shape, BF16),
        vmem(key_cache.shape, BF16),
        vmem(value_cache.shape, BF16),
        vmem((1, width), F32),
        vmem((2,) + policy_in.shape, BF16),
        vmem(policy_out.shape, BF16),
        vmem((1, heads_width), F32),
        vmem((scenes, branch), jnp.int32),
        vmem((scenes, branch), F32),
        vmem((NARROW, scenes, branch, width), BF16),
        vmem((NARROW, 8, branch), F32),
        vmem((scenes, branch, width), F32),
        vmem((3, branch, features), F32),
        vmem((NARROW, scenes, branch, features), BF16),
        vmem((X, scenes, width, branch), BF16),
        vmem((scenes, branch, 2 * heads_width + 128), BF16),
        vmem((NARROW, scenes, share, 2 * heads_width + 128), BF16),
        vmem((scenes, branch, policy_out.shape[1]), F32),
        vmem((scenes, branch, 128), F32),
        vmem((X, scenes, share, cols), BF16),
        vmem((X, scenes, branch, cols), BF16),
        vmem((NARROW, scenes * share, block + 128), BF16),
        vmem((NARROW, scenes * share, block + 128), BF16),
        vmem((Y, 8, 128), F32),
        vmem((NARROW, 8, 128), F32),
        vmem((width, cols), F32),
        vmem((width, cols), BF16),
        vmem((Z - 1, width // Z, cols), BF16),
        vmem((block, 128), F32),
        vmem((block, 128), BF16),
        vmem((X - 1, block // X, 128), BF16),
        vmem((block // X, 128), BF16),
        vmem((Z - 1, block // X, 128), BF16),
        vmem((X, 8, 128), F32),
        vmem((Z, 8, 128), F32),
        pltpu.SemaphoreType.DMA((len(operands),)),
        pltpu.SemaphoreType.DMA((COPIES,)),
        pltpu.SemaphoreType.DMA((COPIES,)),
    ]
    new_latent, grads, policy_out_grad, misc = pl.pallas_call(
        kernel,
        name="imagine",
        out_shape=(
            jax.ShapeDtypeStruct((scenes, branch, width), BF16),
            jax.ShapeDtypeStruct((2, width, heads_width), BF16),
            jax.ShapeDtypeStruct(policy_out.shape, BF16),
            jax.ShapeDtypeStruct((Y, 8, 128), F32),
        ),
        in_specs=[pl.BlockSpec(memory_space=pl.ANY)] * len(operands),
        out_specs=[pl.BlockSpec(memory_space=pltpu.VMEM)] * 4,
        scratch_shapes=scratch,
        compiler_params=pltpu.CompilerParams(
            collective_id=0, has_side_effects=True, vmem_limit_bytes=60 * 2**20
        ),
    )(*operands)
    return (
        new_latent.reshape(rows, width),
        misc[0, 1, :2] / total_rows,
        grads[0],
        grads[1],
        policy_out_grad,
        misc[:, 0, :].reshape(heads_width).astype(BF16),
    )


def solution(mesh):
    placed = (
        P("wide", "narrow"),
        P("wide"),
        P(None, "narrow"),
        P("narrow"),
        P(None, "narrow"),
        P(None, "narrow"),
        P(None, "narrow"),
        P(None, "narrow"),
        P("wide", None, "narrow"),
        P("wide", None, "narrow"),
        P("narrow"),
        P("narrow", None),
        P("narrow", None),
        P(),
        P(),
        P("wide"),
        P("wide"),
    )
    return jax.shard_map(
        per_device,
        mesh=mesh,
        in_specs=placed,
        out_specs=(P("wide", "narrow"), P(), P("narrow", None), P("narrow", None), P(), P()),
        check_vma=False,
    )
```

```python
import functools

import jax
import jax.numpy as jnp
from jax import lax
from jax.experimental import pallas as pl
from jax.experimental.pallas import tpu as pltpu
from jax.sharding import PartitionSpec as P

HD = 128
EPSILON = 1e-05
X, Y, Z = 4, 4, 8
NARROW = 2 * Y
MESH = pl.DeviceIdType.MESH
F32, BF16 = jnp.float32, jnp.bfloat16
COPIES = 256


def nt_dot(left, right):
    return lax.dot_general(left, right, (((1,), (1,)), ((), ())), preferred_element_type=F32)


def dot(left, right):
    return jnp.dot(left, right, preferred_element_type=F32)


def kernel(
    latent_in,
    actions_in,
    table_in,
    gain1_in,
    w_query_in,
    w_key_in,
    w_value_in,
    w_out_in,
    keys_in,
    values_in,
    gain2_in,
    policy_in_in,
    value_in_in,
    policy_out_in,
    value_out_in,
    targets_in,
    returns_in,
    latent_out,
    grads_out,
    policy_out_grad,
    misc_out,
    latent,
    actions,
    table,
    gain1,
    w_qkv,
    w_out,
    keys,
    values,
    gain2,
    heads_w,
    policy_out,
    value_out,
    targets,
    returns,
    normed,
    squares,
    tokens,
    qkv,
    attended,
    gained_t,
    pre_send,
    pre_recv,
    onehot,
    returns_col,
    dpre_send,
    dpre_recv,
    factor_send,
    factor_recv,
    misc_send,
    misc_recv,
    grad_f32,
    grad_send,
    grad_recv,
    block_f32,
    block_send,
    block_recv,
    block_mid,
    block_recv_z,
    misc_x,
    misc_z,
    load_sem,
    send_sem,
    recv_sem,
):
    wide, narrow = lax.axis_index("wide"), lax.axis_index("narrow")
    x, z = wide // Z, lax.rem(wide, Z)
    y, c = narrow // 2, lax.rem(narrow, 2)
    scenes, branch, width = normed.shape[1:]
    total_rows = scenes * branch * X * Z
    full_width = width * NARROW

    def device(dx=0, dy=0, dz=0, dc=0):
        return (
            lax.rem(x + dx, X) * Z + lax.rem(z + dz, Z),
            lax.rem(y + dy, Y) * 2 + lax.rem(c + dc, 2),
        )

    plane = [(dx, dy, dc) for dx in (2, 1, 3, 0) for dy in (2, 1, 3, 0) for dc in (1, 0)]
    plane = [o for o in plane if o != (0, 0, 0)]
    z_steps = (4, 3, 5, 2, 6, 1, 7)
    x_steps = (2, 1, 3)
    y_steps = (2, 1, 3)
    barrier = pltpu.get_barrier_semaphore()
    partners = [device(dx, dy, 0, dc) for dx, dy, dc in plane] + [device(dz=d) for d in z_steps]
    for partner in partners:
        pl.semaphore_signal(barrier, inc=1, device_id=partner, device_id_type=MESH)

    loads = {}

    def load(name, source, target):
        copy = pltpu.make_async_copy(source, target, load_sem.at[len(loads)])
        copy.start()
        loads[name] = copy

    def ready(*names):
        for name in names:
            loads[name].wait()
            loads[name] = None

    load("actions", actions_in, actions)
    load("table", table_in, table)
    load("latent", latent_in, latent)
    load("gain1", gain1_in, gain1)
    load("w_query", w_query_in, w_qkv.at[0])
    load("w_key", w_key_in, w_qkv.at[1])
    load("w_value", w_value_in, w_qkv.at[2])
    load("keys", keys_in, keys)
    load("values", values_in, values)
    load("w_out", w_out_in, w_out)
    load("gain2", gain2_in, gain2)
    load("policy_in", policy_in_in, heads_w.at[0])
    load("value_in", value_in_in, heads_w.at[1])
    load("policy_out", policy_out_in, policy_out)
    load("value_out", value_out_in, value_out)
    load("targets", targets_in, targets)
    load("returns", returns_in, returns)

    started, pending = [], {}

    def send(source, target, partner):
        i = len(started)
        copy = pltpu.make_async_remote_copy(
            src_ref=source,
            dst_ref=target,
            send_sem=send_sem.at[i],
            recv_sem=recv_sem.at[i],
            device_id=partner,
            device_id_type=MESH,
        )
        copy.start()
        started.append(copy)
        pending[id(copy)] = copy
        return copy

    def arrive(*copies):
        for copy in copies:
            copy.wait_recv()
            del pending[id(copy)]

    def finish():
        ready(*[name for name in loads if loads[name] is not None])
        arrive(*list(pending.values()))
        for copy in started:
            copy.wait_send()

    ready("actions", "table", "latent", "gain1")
    action_count = table.shape[0]
    action_ids = lax.broadcasted_iota(jnp.int32, (action_count, branch), 0)
    for s in range(scenes):
        chosen = (actions[s : s + 1, :] == action_ids).astype(F32).T.astype(BF16)
        token = latent[s].astype(F32) + dot(chosen, table[...])
        tokens[s] = token
        normed[narrow, s] = (token * gain1[...]).astype(BF16)
        square = token * token
        square = sum(square[:, i : i + 128] for i in range(0, width, 128))
        squares[narrow, s : s + 1, :] = jnp.sum(square.T, axis=0, keepdims=True)

    pl.semaphore_wait(barrier, len(partners))

    def gather_start(buffer, s):
        own = buffer.at[narrow, s]
        near = send(own, own, device(dc=1))
        far = [send(own, own, device(dy=d)) for d in y_steps]
        return near, far

    def gather_slots(buffer, s, near, far):
        yield narrow
        arrive(near)
        yield y * 2 + 1 - c
        passed = []
        for d, copy in zip(y_steps, far):
            slot = lax.rem(y - d + Y, Y) * 2 + c
            arrive(copy)
            passed.append(send(buffer.at[slot, s], buffer.at[slot, s], device(dc=1)))
            yield slot
        for d, copy in zip(y_steps, passed):
            arrive(copy)
            yield lax.rem(y - d + Y, Y) * 2 + 1 - c

    gathers = [gather_start(normed, 0)]
    square_copies = [
        send(squares.at[narrow], squares.at[narrow], device(dy=dy, dc=dc))
        for dx, dy, dc in plane
        if dx == 0
    ]
    gathers.append(gather_start(normed, 1))

    ready("targets")
    ready("returns")
    for s in range(scenes):
        onehot[s] = (targets[s : s + 1, :] == action_ids).astype(F32).T
        returns_col[s] = jnp.broadcast_to(returns[s : s + 1, :], (128, branch)).T

    ready("w_query", "w_key", "w_value", "keys", "values")
    scaling = HD ** (-0.5)
    heads_local = w_qkv.shape[2] // HD
    attended_copies = []
    for s in range(scenes):
        first = True
        for slot in gather_slots(normed, s, *gathers[s]):
            rows = normed[slot, s]
            for i in range(3):
                product = dot(rows, w_qkv[i, pl.ds(pl.multiple_of(slot * width, width), width), :])
                if first:
                    qkv[i] = product
                else:
                    qkv[i] += product
            first = False
        if s == 0:
            arrive(*square_copies)
        total = jnp.sum(squares[:, s : s + 1, :], axis=0)
        inverse = lax.rsqrt(total / full_width + EPSILON)
        inverse = jnp.broadcast_to(inverse, (128, branch)).T
        for h in range(heads_local):
            cols = slice(h * HD, (h + 1) * HD)
            query, key_new, value_new = ((qkv[i, :, cols] * inverse).astype(BF16) for i in range(3))
            scores = nt_dot(query, keys[s, :, cols]) * scaling
            own_score = (
                jnp.sum(query.astype(F32) * key_new.astype(F32), axis=1, keepdims=True) * scaling
            )
            highest = jnp.maximum(jnp.max(scores, axis=1, keepdims=True), own_score)
            expd = jnp.exp(scores - highest)
            own_exp = jnp.exp(own_score - highest)
            share = 1.0 / (jnp.sum(expd, axis=1, keepdims=True) + own_exp)
            weights = (expd * share).astype(BF16)
            own_weight = (own_exp * share).astype(BF16).astype(F32)
            mixed = dot(weights, values[s, :, cols]) + own_weight * value_new.astype(F32)
            attended[narrow, s, :, cols] = mixed.astype(BF16)
        attended_copies.append(gather_start(attended, s))

    ready("w_out", "gain2", "policy_in", "value_in")
    heads_width = heads_w.shape[2]
    both = 2 * heads_width
    depth = attended.shape[3]
    share_rows = branch // NARROW
    my_rows = pl.ds(pl.multiple_of(narrow * share_rows, share_rows), share_rows)
    pre_copies, state_copies = [], []
    for s in range(scenes):
        for slot in gather_slots(attended, s, *attended_copies[s]):
            tokens[s] += dot(
                attended[slot, s], w_out[pl.ds(pl.multiple_of(slot * depth, depth), depth), :]
            )
        state = tokens[s]
        gained = state * gain2[...]
        gained_b = gained.astype(BF16)
        for i in range(2):
            pre_send[s, :, i * heads_width : (i + 1) * heads_width] = dot(
                gained_b, heads_w[i]
            ).astype(BF16)
        square = jnp.sum(state * state, axis=1, keepdims=True)
        high = square.astype(BF16)
        low = (square - high.astype(F32)).astype(BF16)
        lane = lax.broadcasted_iota(jnp.int32, (branch, 128), 1)
        pre_send[s, :, both:] = jnp.where(lane < 64, high.astype(F32), low.astype(F32)).astype(BF16)
        copies = []
        for dx, dy, dc in plane:
            if dx == 0:
                partner = device(dy=dy, dc=dc)
                rows = pl.ds(pl.multiple_of(partner[1] * share_rows, share_rows), share_rows)
                copies.append(send(pre_send.at[s, rows], pre_recv.at[narrow, s], partner))
        pre_copies.append(copies)
        pre_recv[narrow, s] = pre_send[s, my_rows, :]
        latent_out[s] = state.astype(BF16)
        gained_t[x, s] = gained.T.astype(BF16)
        state_copies.append(
            [send(gained_t.at[x, s], gained_t.at[x, s], device(dx=d)) for d in x_steps]
        )

    ready("policy_out")
    ready("value_out")
    for copies in pre_copies:
        arrive(*copies)
    sums = jnp.concatenate(
        [sum(pre_recv[i, s].astype(F32) for i in range(NARROW)) for s in range(scenes)], axis=0
    )
    square = sums[:, both : both + 1] + sums[:, both + 64 : both + 65]
    inverse = lax.rsqrt(square / full_width + EPSILON)
    pre = sums[:, :both] * inverse
    sigma = 1.0 / (1.0 + jnp.exp(-pre))
    hidden = (pre * sigma).astype(BF16)
    slope = sigma * (1.0 + pre * (1.0 - sigma))
    policy_hidden, value_hidden = hidden[:, :heads_width], hidden[:, heads_width:].astype(F32)
    logits = dot(policy_hidden, policy_out[...])
    value_row = value_out[...].astype(F32)
    value_row = jnp.concatenate([value_row[i : i + 1] for i in range(Y)], axis=1)
    value = jnp.sum(value_hidden * value_row, axis=1, keepdims=True)
    top = jnp.max(logits, axis=1, keepdims=True)
    log_total = top + jnp.log(jnp.sum(jnp.exp(logits - top), axis=1, keepdims=True))
    target = jnp.concatenate([onehot[s, my_rows, :] for s in range(scenes)], axis=0)
    wanted = jnp.concatenate([returns_col[s, my_rows, :] for s in range(scenes)], axis=0)
    picked = jnp.sum(logits * target, axis=1, keepdims=True)
    errors = value - wanted[:, 0:1]
    factor = total_rows ** (-0.5)
    dlogits = ((jnp.exp(logits - log_total) - target) * factor).astype(BF16)
    dvalue = (errors * factor).astype(BF16).astype(F32)
    dhidden = nt_dot(dlogits, policy_out[...])
    dpre_policy = (dhidden * slope[:, :heads_width] * inverse).astype(BF16)
    dpre_value = (dvalue * value_row * slope[:, heads_width:] * inverse).astype(BF16)
    dpre = jnp.concatenate([dpre_policy, dpre_value], axis=1)
    cols = both // X
    for i in range(X):
        for s in range(scenes):
            dpre_send[i, s] = dpre[s * share_rows : (s + 1) * share_rows, i * cols : (i + 1) * cols]
    dpre_recv[x, :, my_rows, :] = dpre_send[x]
    dpre_copies = []
    for dx, dy, dc in plane:
        dpre_copies.append(
            send(
                dpre_send.at[lax.rem(x + dx, X)],
                dpre_recv.at[x, :, my_rows, :],
                device(dx=dx, dy=dy, dc=dc),
            )
        )

    block = heads_width // Y
    lanes = lax.broadcasted_iota(jnp.int32, (1, 128), 1)
    sum_policy = jnp.sum(log_total - picked, axis=0, keepdims=True)
    sum_value = 0.5 * jnp.sum(errors * errors, axis=0, keepdims=True)
    loss_row = jnp.where(lanes == 0, sum_policy, jnp.where(lanes == 1, sum_value, 0.0))
    value_grad = jnp.sum(dvalue * value_hidden, axis=0, keepdims=True)
    for i in range(Y):
        for j in range(2):
            factor_send[2 * i + j, :, :block] = policy_hidden[:, i * block : (i + 1) * block]
            factor_send[2 * i + j, :, block:] = dlogits[:, j * 128 : (j + 1) * 128]
        misc_send[i] = jnp.concatenate(
            [value_grad[:, i * block : (i + 1) * block], loss_row, jnp.zeros((6, 128), F32)], axis=0
        )
    factor_recv[narrow] = factor_send[narrow]
    misc_recv[narrow] = misc_send[y]
    factor_copies = []
    for dx, dy, dc in plane:
        if dx == 0:
            partner = device(dy=dy, dc=dc)
            factor_copies.append(send(factor_send.at[partner[1]], factor_recv.at[narrow], partner))
            factor_copies.append(
                send(misc_send.at[lax.rem(y + dy, Y)], misc_recv.at[narrow], partner)
            )

    for copies in state_copies:
        arrive(*copies)
    arrive(*dpre_copies)
    grad = None
    for i in range(X):
        for s in range(scenes):
            product = dot(gained_t[i, s], dpre_recv[i, s])
            grad = product if grad is None else grad + product
    grad_f32[...] = grad
    half = cols // 2
    for i in range(2):
        grad_send[i] = grad[:, i * half : (i + 1) * half].astype(BF16)
    grad_rows = width // Z
    grad_copies = []
    for i in range(2):
        copies = []
        for d in z_steps:
            rows = pl.ds(pl.multiple_of(lax.rem(z + d, Z) * grad_rows, grad_rows), grad_rows)
            copies.append(send(grad_send.at[i, rows], grad_recv.at[i, d - 1], device(dz=d)))
        grad_copies.append(copies)

    arrive(*factor_copies)
    left = jnp.concatenate([factor_recv[i, :, :block] for i in range(NARROW)], axis=0)
    right = jnp.concatenate([factor_recv[i, :, block:] for i in range(NARROW)], axis=0)
    part = dot(left.astype(F32).T.astype(BF16), right)
    block_f32[...] = part
    block_send[...] = part.astype(BF16)
    misc_x[0] = sum(misc_recv[i] for i in range(NARROW))
    block_rows = block // X
    block_copies = []
    for d in x_steps:
        rows = pl.ds(pl.multiple_of(lax.rem(x + d, X) * block_rows, block_rows), block_rows)
        block_copies.append(send(block_send.at[rows], block_recv.at[d - 1], device(dx=d)))
        block_copies.append(send(misc_x.at[0], misc_x.at[d], device(dx=d)))

    arrive(*block_copies)
    my_block = pl.ds(pl.multiple_of(x * block_rows, block_rows), block_rows)
    block_sum = block_f32[my_block, :] + sum(block_recv[i].astype(F32) for i in range(X - 1))
    block_mid[...] = block_sum.astype(BF16)
    misc_z[0] = sum(misc_x[i] for i in range(X))
    block_copies = []
    for d in z_steps:
        block_copies.append(send(block_mid, block_recv_z.at[d - 1], device(dz=d)))
        block_copies.append(send(misc_z.at[0], misc_z.at[d], device(dz=d)))

    my_grad = pl.ds(pl.multiple_of(z * grad_rows, grad_rows), grad_rows)

    def spread(i, rows, **step):
        my_cols = pl.ds(pl.multiple_of(lax.rem(x, 2) * cols + i * half, half), half)
        place = grads_out.at[x // 2, rows, my_cols]
        return send(place, place, device(**step))

    along_z, along_x = [], []
    for i in range(2):
        arrive(*grad_copies[i])
        reduced = grad_f32[my_grad, i * half : (i + 1) * half]
        reduced = reduced + sum(grad_recv[i, j].astype(F32) for j in range(Z - 1))
        my_cols = pl.ds(pl.multiple_of(lax.rem(x, 2) * cols + i * half, half), half)
        grads_out[x // 2, my_grad, my_cols] = reduced.astype(BF16)
        along_z.append({d: spread(i, my_grad, dz=d) for d in z_steps})
        along_x.extend(spread(i, my_grad, dx=d) for d in x_steps)

    def forward(i, *steps):
        for d in steps:
            arrive(along_z[i][d])
            rows = pl.ds(pl.multiple_of(lax.rem(z - d + Z, Z) * grad_rows, grad_rows), grad_rows)
            along_x.extend(spread(i, rows, dx=e) for e in x_steps)

    arrive(*block_copies)
    reduced = block_sum + sum(block_recv_z[i].astype(F32) for i in range(Z - 1))
    block_cols = pl.ds(pl.multiple_of(c * 128, 128), 128)
    place = policy_out_grad.at[
        pl.ds(pl.multiple_of(y * block + x * block_rows, block_rows), block_rows), block_cols
    ]
    place[...] = reduced.astype(BF16)
    block_copies = [send(place, place, device(dx=d)) for d in x_steps]
    misc_out[y] = sum(misc_z[i] for i in range(Z))
    misc_copies = [send(misc_out.at[y], misc_out.at[y], device(dy=d)) for d in y_steps]
    forward(0, 1, 7, 2, 6)
    arrive(*block_copies)
    place = policy_out_grad.at[pl.ds(pl.multiple_of(y * block, block), block), block_cols]
    block_copies = [send(place, place, device(dy=dy, dc=dc)) for dx, dy, dc in plane if dx == 0]
    forward(0, 3, 5, 4)
    forward(1, 1, 7, 2, 6, 3, 5, 4)
    finish()


def deliver(
    total_rows,
    latent,
    grads,
    policy_out_grad,
    misc,
    latent_to,
    policy_in_to,
    value_in_to,
    policy_out_to,
    losses_to,
    value_out_to,
    losses,
    value_out_grad,
    sem,
):
    copies = [
        pltpu.make_async_copy(source, target, sem.at[i])
        for i, (source, target) in enumerate(
            (
                (grads.at[0], policy_in_to),
                (grads.at[1], value_in_to),
                (latent, latent_to),
                (policy_out_grad, policy_out_to),
                (losses, losses_to),
                (value_out_grad, value_out_to),
            )
        )
    ]
    for copy in copies[:4]:
        copy.start()
    losses[...] = misc[0, 1:2, :2] * (1.0 / total_rows)
    value_out_grad[...] = jnp.concatenate(
        [misc[i, 0:1, :] for i in range(misc.shape[0])], axis=0
    ).astype(BF16)
    for copy in copies[4:]:
        copy.start()
    for copy in copies:
        copy.wait()


def per_device(
    latent,
    actions,
    action_table,
    norm1_gain,
    w_query,
    w_key,
    w_value,
    w_out,
    key_cache,
    value_cache,
    norm2_gain,
    policy_in,
    value_in,
    policy_out,
    value_out,
    targets,
    returns,
):
    rows, width = latent.shape
    scenes = key_cache.shape[0]
    branch = rows // scenes
    heads_width = policy_in.shape[1]
    features = w_query.shape[1]
    share = branch // NARROW
    block = heads_width // Y
    cols = 2 * heads_width // X
    total_rows = rows * X * Z
    vmem = pltpu.VMEM
    operands = (
        latent.reshape(scenes, branch, width),
        actions.reshape(scenes, branch),
        action_table,
        norm1_gain.reshape(1, width),
        w_query,
        w_key,
        w_value,
        w_out,
        key_cache,
        value_cache,
        norm2_gain.reshape(1, width),
        policy_in,
        value_in,
        policy_out,
        value_out.reshape(Y, 128),
        targets.reshape(scenes, branch),
        returns.reshape(scenes, branch),
    )
    operands = [pltpu.with_memory_space_constraint(operand, pltpu.HBM) for operand in operands]
    scratch = [
        vmem((scenes, branch, width), BF16),
        vmem((scenes, branch), jnp.int32),
        vmem(action_table.shape, BF16),
        vmem((1, width), F32),
        vmem((3,) + w_query.shape, BF16),
        vmem(w_out.shape, BF16),
        vmem(key_cache.shape, BF16),
        vmem(value_cache.shape, BF16),
        vmem((1, width), F32),
        vmem((2,) + policy_in.shape, BF16),
        vmem(policy_out.shape, BF16),
        vmem((Y, 128), BF16),
        vmem((scenes, branch), jnp.int32),
        vmem((scenes, branch), F32),
        vmem((NARROW, scenes, branch, width), BF16),
        vmem((NARROW, 8, branch), F32),
        vmem((scenes, branch, width), F32),
        vmem((3, branch, features), F32),
        vmem((NARROW, scenes, branch, features), BF16),
        vmem((X, scenes, width, branch), BF16),
        vmem((scenes, branch, 2 * heads_width + 128), BF16),
        vmem((NARROW, scenes, share, 2 * heads_width + 128), BF16),
        vmem((scenes, branch, policy_out.shape[1]), F32),
        vmem((scenes, branch, 128), F32),
        vmem((X, scenes, share, cols), BF16),
        vmem((X, scenes, branch, cols), BF16),
        vmem((NARROW, scenes * share, block + 128), BF16),
        vmem((NARROW, scenes * share, block + 128), BF16),
        vmem((Y, 8, 128), F32),
        vmem((NARROW, 8, 128), F32),
        vmem((width, cols), F32),
        vmem((2, width, cols // 2), BF16),
        vmem((2, Z - 1, width // Z, cols // 2), BF16),
        vmem((block, 128), F32),
        vmem((block, 128), BF16),
        vmem((X - 1, block // X, 128), BF16),
        vmem((block // X, 128), BF16),
        vmem((Z - 1, block // X, 128), BF16),
        vmem((X, 8, 128), F32),
        vmem((Z, 8, 128), F32),
        pltpu.SemaphoreType.DMA((len(operands),)),
        pltpu.SemaphoreType.DMA((COPIES,)),
        pltpu.SemaphoreType.DMA((COPIES,)),
    ]
    results = pl.pallas_call(
        kernel,
        name="imagine",
        out_shape=(
            vmem((scenes, branch, width), BF16),
            vmem((2, width, heads_width), BF16),
            vmem(policy_out.shape, BF16),
            vmem((Y, 8, 128), F32),
        ),
        in_specs=[pl.BlockSpec(memory_space=pltpu.HBM)] * len(operands),
        out_specs=[pl.BlockSpec(memory_space=pltpu.VMEM)] * 4,
        scratch_shapes=scratch,
        compiler_params=pltpu.CompilerParams(
            collective_id=0, has_side_effects=True, vmem_limit_bytes=40 * 2**20
        ),
    )(*operands)
    new_latent, policy_in_grad, value_in_grad, policy_out_grad, losses, value_out_grad = pl.pallas_call(
        functools.partial(deliver, total_rows),
        name="deliver",
        out_shape=(
            jax.ShapeDtypeStruct((scenes, branch, width), BF16),
            jax.ShapeDtypeStruct(policy_in.shape, BF16),
            jax.ShapeDtypeStruct(value_in.shape, BF16),
            jax.ShapeDtypeStruct(policy_out.shape, BF16),
            jax.ShapeDtypeStruct((1, 2), F32),
            jax.ShapeDtypeStruct((Y, 128), BF16),
        ),
        in_specs=[pl.BlockSpec(memory_space=pltpu.VMEM)] * 4,
        out_specs=[pl.BlockSpec(memory_space=pltpu.HBM)] * 6,
        scratch_shapes=[
            vmem((1, 2), F32),
            vmem((Y, 128), BF16),
            pltpu.SemaphoreType.DMA((6,)),
        ],
        compiler_params=pltpu.CompilerParams(vmem_limit_bytes=8 * 2**20),
    )(*[pltpu.with_memory_space_constraint(result, pltpu.VMEM) for result in results])
    return (
        new_latent.reshape(rows, width),
        losses.reshape(2),
        policy_in_grad,
        value_in_grad,
        policy_out_grad,
        value_out_grad.reshape(heads_width),
    )


def solution(mesh):
    placed = (
        P("wide", "narrow"),
        P("wide"),
        P(None, "narrow"),
        P("narrow"),
        P(None, "narrow"),
        P(None, "narrow"),
        P(None, "narrow"),
        P(None, "narrow"),
        P("wide", None, "narrow"),
        P("wide", None, "narrow"),
        P("narrow"),
        P("narrow", None),
        P("narrow", None),
        P(),
        P(),
        P("wide"),
        P("wide"),
    )
    return jax.shard_map(
        per_device,
        mesh=mesh,
        in_specs=placed,
        out_specs=(P("wide", "narrow"), P(), P("narrow", None), P("narrow", None), P(), P()),
        check_vma=False,
    )
```

```python
import functools

import jax
import jax.numpy as jnp
from jax import lax
from jax.experimental import pallas as pl
from jax.experimental.pallas import tpu as pltpu
from jax.sharding import PartitionSpec as P

HD = 128
EPSILON = 1e-05
X, Y, Z = 4, 4, 8
NARROW = 2 * Y
MESH = pl.DeviceIdType.MESH
F32, BF16 = jnp.float32, jnp.bfloat16
LOADS, SENDS, ARRIVALS = 14, 19, 75


def nt_dot(left, right):
    return lax.dot_general(left, right, (((1,), (1,)), ((), ())), preferred_element_type=F32)


def dot(left, right):
    return jnp.dot(left, right, preferred_element_type=F32)


def kernel(
    latent_in,
    actions_in,
    table_in,
    gain1_in,
    w_query_in,
    w_key_in,
    w_value_in,
    w_out_in,
    keys_in,
    values_in,
    gain2_in,
    policy_in_in,
    value_in_in,
    policy_out_in,
    value_out_in,
    targets_in,
    returns_in,
    latent_out,
    grads_out,
    policy_out_grad,
    misc_out,
    latent,
    actions,
    table,
    gain1,
    w_qkv,
    w_out,
    keys,
    values,
    gain2,
    heads_w,
    policy_out,
    value_out,
    targets,
    returns,
    normed,
    squares,
    tokens,
    qkv,
    attended,
    gained_t,
    pre_send,
    pre_recv,
    onehot,
    returns_col,
    dpre_send,
    dpre_recv,
    factor_send,
    factor_recv,
    misc_send,
    misc_recv,
    grad_f32,
    grad_send,
    grad_recv,
    block_f32,
    block_send,
    block_recv,
    block_mid,
    block_recv_z,
    misc_x,
    misc_z,
    load_sem,
    send_sem,
    recv_sem,
):
    wide, narrow = lax.axis_index("wide"), lax.axis_index("narrow")
    x, z = wide // Z, lax.rem(wide, Z)
    y, c = narrow // 2, lax.rem(narrow, 2)
    _, scenes, branch, width = normed.shape
    total_rows = scenes * branch * X * Z
    full_width = width * NARROW

    def device(dx=0, dy=0, dz=0, dc=0):
        return (
            lax.rem(x + dx, X) * Z + lax.rem(z + dz, Z),
            lax.rem(y + dy, Y) * 2 + lax.rem(c + dc, 2),
        )

    def span(index, size):
        return pl.ds(pl.multiple_of(index * size, size), size)

    plane = [(dx, dy, dc) for dx in (2, 1, 3, 0) for dy in (2, 1, 3, 0) for dc in (1, 0)]
    plane = [o for o in plane if o != (0, 0, 0)]
    line = [(dy, dc) for dx, dy, dc in plane if dx == 0]
    z_steps = (4, 3, 5, 2, 6, 1, 7)
    x_steps = (2, 1, 3)
    y_steps = (2, 1, 3)
    barrier = pltpu.get_barrier_semaphore()
    partners = [device(dx, dy, 0, dc) for dx, dy, dc in plane] + [device(dz=d) for d in z_steps]
    for partner in partners:
        pl.semaphore_signal(barrier, inc=1, device_id=partner, device_id_type=MESH)

    places = [narrow, y * 2 + 1 - c]
    places += [lax.rem(y - d + Y, Y) * 2 + c for d in y_steps]
    places += [lax.rem(y - d + Y, Y) * 2 + 1 - c for d in y_steps]

    loads = {}

    def load(name, target, *pieces):
        sem = load_sem.at[len(loads)]
        for source, part in pieces:
            pltpu.make_async_copy(source, part, sem).start()
        loads[name] = pltpu.make_async_copy(target, target, sem)

    def ready(*names):
        for name in names:
            loads[name].wait()
            loads[name] = None

    load("actions", actions, (actions_in, actions))
    load("table", table, (table_in, table))
    load("latent", latent, (latent_in, latent))
    load("gain1", gain1, (gain1_in, gain1))
    weights = (w_query_in, w_key_in, w_value_in)
    load(
        "w_qkv",
        w_qkv,
        *[
            (weights[i].at[span(place, width)], w_qkv.at[i, pl.ds(p * width, width)])
            for p, place in enumerate(places)
            for i in range(3)
        ],
    )
    load("keys", keys, (keys_in, keys))
    load("values", values, (values_in, values))
    depth = w_qkv.shape[2]
    load(
        "w_out",
        w_out,
        *[
            (w_out_in.at[span(place, depth)], w_out.at[pl.ds(p * depth, depth)])
            for p, place in enumerate(places)
        ],
    )
    load("gain2", gain2, (gain2_in, gain2))
    load("heads_w", heads_w, (policy_in_in, heads_w.at[0]), (value_in_in, heads_w.at[1]))
    load("policy_out", policy_out, (policy_out_in, policy_out))
    load("value_out", value_out, (value_out_in, value_out))
    load("targets", targets, (targets_in, targets))
    load("returns", returns, (returns_in, returns))

    started, pending, groups, outgoing = [], {}, {}, {}
    counts = [0]

    def group_sem(name):
        if name not in groups:
            groups[name] = (counts[0], [])
            counts[0] += 1
        return recv_sem.at[groups[name][0]]

    def send(source, target, partner, out, into=None):
        if out not in outgoing:
            outgoing[out] = len(outgoing)
        if into is None:
            arrival = recv_sem.at[counts[0]]
            counts[0] += 1
        else:
            arrival = group_sem(into)
        copy = pltpu.make_async_remote_copy(
            src_ref=source,
            dst_ref=target,
            send_sem=send_sem.at[outgoing[out]],
            recv_sem=arrival,
            device_id=partner,
            device_id_type=MESH,
        )
        copy.start()
        started.append(copy)
        if into is None:
            pending[id(copy)] = copy
        else:
            groups[into][1].append(copy)
        return copy

    def arrive(*copies):
        for copy in copies:
            copy.wait_recv()
            del pending[id(copy)]

    def collect(name, whole):
        pltpu.make_async_copy(whole, whole, recv_sem.at[groups[name][0]]).wait()
        groups[name][1].clear()

    def finish(whole=None):
        ready(*[name for name in loads if loads[name] is not None])
        arrive(*list(pending.values()))
        if whole is None:
            for copies in groups.values():
                for copy in copies[1]:
                    copy.wait_recv()
            for copy in started:
                copy.wait_send()
        else:
            for name, i in outgoing.items():
                pltpu.make_async_copy(whole[name], whole[name], send_sem.at[i]).wait()

    ready("actions", "table", "latent", "gain1")
    action_count = table.shape[0]
    action_ids = lax.broadcasted_iota(jnp.int32, (action_count, branch), 0)
    for s in range(scenes):
        chosen = (actions[s : s + 1, :] == action_ids).astype(F32).T.astype(BF16)
        token = latent[s].astype(F32) + dot(chosen, table[...])
        tokens[s] = token
        normed[0, s] = (token * gain1[...]).astype(BF16)
        square = token * token
        square = sum(square[:, i : i + 128] for i in range(0, width, 128))
        squares[0, s : s + 1, :] = jnp.sum(square.T, axis=0, keepdims=True)

    pl.semaphore_wait(barrier, len(partners))

    def gather_start(buffer, s, out):
        near = send(buffer.at[0, s], buffer.at[1, s], device(dc=1), out)
        far = [
            send(buffer.at[0, s], buffer.at[2 + i, s], device(dy=d), out)
            for i, d in enumerate(y_steps)
        ]
        return near, far

    def gather_pass(buffer, s, far, out):
        passed = []
        for i, copy in enumerate(far):
            arrive(copy)
            passed.append(send(buffer.at[2 + i, s], buffer.at[5 + i, s], device(dc=1), out))
        return passed

    def gathered(buffer, s, low, high):
        return jnp.concatenate([buffer[p, s] for p in range(low, high)], axis=1)

    gathers = [gather_start(normed, 0, "normed")]
    for dy, dc in line:
        send(squares.at[0], squares.at[2 * dy + dc], device(dy=dy, dc=dc), "squares", "squares")
    gathers.append(gather_start(normed, 1, "normed"))

    ready("targets", "returns")
    for s in range(scenes):
        onehot[s] = (targets[s : s + 1, :] == action_ids).astype(F32).T
        returns_col[s] = jnp.broadcast_to(returns[s : s + 1, :], (128, branch)).T

    scaling = HD ** (-0.5)
    heads_local = depth // HD
    attended_copies = []

    def project(s, low, high):
        rows = gathered(normed, s, low, high)
        for i in range(3):
            product = dot(rows, w_qkv[i, low * width : high * width, :])
            if low == 0:
                qkv[s, i] = product
            else:
                qkv[s, i] += product

    ready("w_qkv")
    for s in range(scenes):
        arrive(gathers[s][0])
        project(s, 0, 2)
    for s in range(scenes):
        passed = gather_pass(normed, s, gathers[s][1], "normed")
        project(s, 2, 5)
        arrive(*passed)
        project(s, 5, 8)
        if s == 0:
            collect("squares", squares.at[pl.ds(1, NARROW - 1)])
            ready("keys", "values")
        total = jnp.sum(squares[:, s : s + 1, :], axis=0)
        inverse = lax.rsqrt(total / full_width + EPSILON)
        inverse = jnp.broadcast_to(inverse, (128, branch)).T
        for h in range(heads_local):
            cols = slice(h * HD, (h + 1) * HD)
            query, key_new, value_new = (
                (qkv[s, i, :, cols] * inverse).astype(BF16) for i in range(3)
            )
            scores = nt_dot(query, keys[s, :, cols]) * scaling
            own_score = (
                jnp.sum(query.astype(F32) * key_new.astype(F32), axis=1, keepdims=True) * scaling
            )
            highest = jnp.maximum(jnp.max(scores, axis=1, keepdims=True), own_score)
            expd = jnp.exp(scores - highest)
            own_exp = jnp.exp(own_score - highest)
            share = 1.0 / (jnp.sum(expd, axis=1, keepdims=True) + own_exp)
            probs = (expd * share).astype(BF16)
            own_prob = (own_exp * share).astype(BF16).astype(F32)
            mixed = dot(probs, values[s, :, cols]) + own_prob * value_new.astype(F32)
            attended[0, s, :, cols] = mixed.astype(BF16)
        attended_copies.append(gather_start(attended, s, "attended"))

    ready("w_out", "gain2", "heads_w")
    heads_width = heads_w.shape[2]
    both = 2 * heads_width
    share_rows = branch // NARROW
    my_rows = span(narrow, share_rows)
    for s in range(scenes):
        near, far = attended_copies[s]

        def update(low, high):
            return dot(gathered(attended, s, low, high), w_out[low * depth : high * depth, :])

        arrive(near)
        tokens[s] += update(0, 2)
        passed = gather_pass(attended, s, far, "attended")
        tokens[s] += update(2, 5)
        arrive(*passed)
        state = tokens[s] + update(5, 8)
        gained = state * gain2[...]
        gained_b = gained.astype(BF16)
        for i in range(2):
            pre_send[s, :, i * heads_width : (i + 1) * heads_width] = dot(
                gained_b, heads_w[i]
            ).astype(BF16)
        square = jnp.sum(state * state, axis=1, keepdims=True)
        high = square.astype(BF16).astype(F32)
        lane = lax.broadcasted_iota(jnp.int32, (branch, 128), 1)
        pre_send[s, :, both:] = jnp.where(lane < 64, high, square - high).astype(BF16)
        for dy, dc in line:
            partner = device(dy=dy, dc=dc)
            send(
                pre_send.at[s, span(partner[1], share_rows)],
                pre_recv.at[s, 2 * dy + dc],
                partner,
                "pre",
                ("pre", s),
            )
        pre_recv[s, 0] = pre_send[s, my_rows, :]
        latent_out[s] = state.astype(BF16)
        gained_t[0, s] = gained.T.astype(BF16)
        for d in x_steps:
            send(gained_t.at[0, s], gained_t.at[d, s], device(dx=d), "gained", "gained")

    ready("policy_out", "value_out")
    for s in range(scenes):
        collect(("pre", s), pre_recv.at[s, pl.ds(1, NARROW - 1)])

    def summed(low, high):
        return jnp.concatenate(
            [
                sum(pre_recv[s, i, :, low:high].astype(F32) for i in range(NARROW))
                for s in range(scenes)
            ],
            axis=0,
        )

    square = summed(both, both + 128)
    square = square[:, 0:1] + square[:, 64:65]
    inverse = lax.rsqrt(square / full_width + EPSILON)

    def hidden_layer(low):
        pre = summed(low, low + heads_width) * inverse
        sigma = 1.0 / (1.0 + jnp.exp(-pre))
        slope = sigma * (1.0 + pre * (1.0 - sigma)) * inverse
        return (pre * sigma).astype(BF16), slope

    half = heads_width // X

    def share_dpre(i, dpre):
        for j in range(X):
            for s in range(scenes):
                dpre_send[i, j, s] = dpre[
                    s * share_rows : (s + 1) * share_rows, j * half : (j + 1) * half
                ]
        own = pltpu.make_async_copy(
            dpre_send.at[i, x], dpre_recv.at[i, 0, :, my_rows, :], group_sem(("dpre", i))
        )
        own.start()
        for dx, dy, dc in plane:
            send(
                dpre_send.at[i, lax.rem(x + dx, X)],
                dpre_recv.at[i, dx, :, my_rows, :],
                device(dx=dx, dy=dy, dc=dc),
                "dpre_y" if dx == 0 else "dpre_x",
                ("dpre", i),
            )

    factor = total_rows ** (-0.5)
    hidden, slope = hidden_layer(heads_width)
    value_hidden = hidden.astype(F32)
    value_row = value_out[...].astype(F32)
    value_row = jnp.concatenate([value_row[i : i + 1] for i in range(Y)], axis=1)
    value = jnp.sum(value_hidden * value_row, axis=1, keepdims=True)
    wanted = jnp.concatenate([returns_col[s, my_rows, :] for s in range(scenes)], axis=0)
    errors = value - wanted[:, 0:1]
    dvalue = (errors * factor).astype(BF16).astype(F32)
    share_dpre(0, (dvalue * value_row * slope).astype(BF16))

    policy_hidden, slope = hidden_layer(0)
    logits = dot(policy_hidden, policy_out[...])
    top = jnp.max(logits, axis=1, keepdims=True)
    log_total = top + jnp.log(jnp.sum(jnp.exp(logits - top), axis=1, keepdims=True))
    target = jnp.concatenate([onehot[s, my_rows, :] for s in range(scenes)], axis=0)
    dlogits = ((jnp.exp(logits - log_total) - target) * factor).astype(BF16)
    share_dpre(1, (nt_dot(dlogits, policy_out[...]) * slope).astype(BF16))

    block = heads_width // Y
    lanes = lax.broadcasted_iota(jnp.int32, (1, 128), 1)
    picked = jnp.sum(logits * target, axis=1, keepdims=True)
    sum_policy = jnp.sum(log_total - picked, axis=0, keepdims=True)
    sum_value = 0.5 * jnp.sum(errors * errors, axis=0, keepdims=True)
    loss_row = jnp.where(lanes == 0, sum_policy, jnp.where(lanes == 1, sum_value, 0.0))
    value_grad = jnp.sum(dvalue * value_hidden, axis=0, keepdims=True)
    for i in range(Y):
        for j in range(2):
            factor_send[2 * i + j, :, :block] = policy_hidden[:, i * block : (i + 1) * block]
            factor_send[2 * i + j, :, block:] = dlogits[:, j * 128 : (j + 1) * 128]
        misc_send[i] = jnp.concatenate(
            [value_grad[:, i * block : (i + 1) * block], loss_row, jnp.zeros((6, 128), F32)], axis=0
        )
    factor_recv[0] = factor_send[narrow]
    misc_recv[0] = misc_send[y]
    for dy, dc in line:
        partner, i = device(dy=dy, dc=dc), 2 * dy + dc
        send(factor_send.at[partner[1]], factor_recv.at[i], partner, "factor", "factor")
        send(misc_send.at[lax.rem(y + dy, Y)], misc_recv.at[i], partner, "misc", "misc")

    collect("gained", gained_t.at[pl.ds(1, X - 1)])
    state_t = jnp.concatenate(
        [gained_t[i, s] for i in range(X) for s in range(scenes)], axis=1
    )
    grad_rows = width // Z
    my_grad = span(z, grad_rows)
    for i in range(2):
        collect(("dpre", i), dpre_recv.at[i])
        grad = dot(
            state_t,
            jnp.concatenate([dpre_recv[i, j, s] for j in range(X) for s in range(scenes)], axis=0),
        )
        grad_f32[i] = grad
        grad_send[i] = grad.astype(BF16)
        for d in z_steps:
            rows = span(lax.rem(z + d, Z), grad_rows)
            send(
                grad_send.at[i, rows], grad_recv.at[i, d - 1], device(dz=d), "grad", ("grad", i)
            )

    collect("factor", factor_recv.at[pl.ds(1, NARROW - 1)])
    collect("misc", misc_recv.at[pl.ds(1, NARROW - 1)])
    left = jnp.concatenate([factor_recv[i, :, :block] for i in range(NARROW)], axis=0)
    right = jnp.concatenate([factor_recv[i, :, block:] for i in range(NARROW)], axis=0)
    part = dot(left.astype(F32).T.astype(BF16), right)
    block_f32[...] = part
    block_send[...] = part.astype(BF16)
    misc_x[0] = sum(misc_recv[i] for i in range(NARROW))
    block_rows = block // X
    for d in x_steps:
        rows = span(lax.rem(x + d, X), block_rows)
        send(block_send.at[rows], block_recv.at[d - 1], device(dx=d), "block", "block")
        send(misc_x.at[0], misc_x.at[d], device(dx=d), "misc_x", "misc_x")

    def spread(i, rows, out, into=None, **step):
        place = grads_out.at[1 - i, rows, span(x, half)]
        return send(place, place, device(**step), out, into)

    def spread_x(i, rows):
        for d in x_steps:
            spread(i, rows, "x", ("x", i, d), dx=d)

    along_z = []
    for i in range(2):
        collect(("grad", i), grad_recv.at[i])
        reduced = grad_f32[i, my_grad, :] + sum(grad_recv[i, j].astype(F32) for j in range(Z - 1))
        grads_out[1 - i, my_grad, span(x, half)] = reduced.astype(BF16)
        along_z.append({d: spread(i, my_grad, "z", dz=d) for d in z_steps})
        spread_x(i, my_grad)
        if i == 0:
            collect("block", block_recv)
            collect("misc_x", misc_x.at[pl.ds(1, X - 1)])
            block_sum = block_f32[span(x, block_rows), :]
            block_sum = block_sum + sum(block_recv[j].astype(F32) for j in range(X - 1))
            block_mid[...] = block_sum.astype(BF16)
            misc_z[0] = sum(misc_x[j] for j in range(X))
            for d in z_steps:
                send(block_mid, block_recv_z.at[d - 1], device(dz=d), "block_z", "block_z")
                send(misc_z.at[0], misc_z.at[d], device(dz=d), "misc_z", "misc_z")

    def forward(i, *steps):
        for d in steps:
            arrive(along_z[i][d])
            spread_x(i, span(lax.rem(z - d + Z, Z), grad_rows))

    forward(0, 1, 7, 2, 6)
    collect("block_z", block_recv_z)
    collect("misc_z", misc_z.at[pl.ds(1, Z - 1)])
    reduced = block_sum + sum(block_recv_z[i].astype(F32) for i in range(Z - 1))
    block_cols = span(c, 128)
    place = policy_out_grad.at[span(y * X + x, block_rows), block_cols]
    place[...] = reduced.astype(BF16)
    block_copies = [send(place, place, device(dx=d), "block_x") for d in x_steps]
    misc_out[y] = sum(misc_z[i] for i in range(Z))
    for d in y_steps:
        send(misc_out.at[y], misc_out.at[y], device(dy=d), "misc_y")
    forward(0, 3, 5, 4)
    arrive(*block_copies)
    place = policy_out_grad.at[span(y, block), block_cols]
    for dy, dc in line:
        send(place, place, device(dy=dy, dc=dc), "block_y")
    forward(1, 1, 7, 2, 6, 3, 5, 4)
    for i in range(2):
        for d in x_steps:
            collect(("x", i, d), grads_out.at[1 - i, :, span(lax.rem(x - d + X, X), half)])
    finish(
        {
            "normed": normed.at[pl.ds(0, 7)],
            "squares": squares.at[pl.ds(0, 7)],
            "attended": attended.at[pl.ds(0, 7)],
            "pre": pre_recv.at[:, pl.ds(0, 7)],
            "gained": gained_t.at[pl.ds(0, 3)],
            "dpre_x": dpre_recv.at[:, pl.ds(0, 3)],
            "dpre_y": dpre_recv.at[:, 0, :, pl.ds(0, 7 * share_rows), :],
            "factor": factor_recv.at[pl.ds(0, 7)],
            "misc": misc_recv.at[pl.ds(0, 7)],
            "grad": grad_recv,
            "block": block_recv,
            "misc_x": misc_x.at[pl.ds(0, 3)],
            "z": grads_out.at[:, pl.ds(0, 112), :],
            "x": grads_out.at[:, pl.ds(0, 384), :],
            "block_z": block_recv_z,
            "misc_z": misc_z.at[pl.ds(0, 7)],
            "block_x": policy_out_grad.at[pl.ds(0, 48)],
            "misc_y": misc_out.at[pl.ds(0, 3)],
            "block_y": policy_out_grad.at[pl.ds(0, 448)],
        }
    )


def deliver(
    total_rows,
    latent,
    grads,
    policy_out_grad,
    misc,
    latent_to,
    policy_in_to,
    value_in_to,
    policy_out_to,
    losses_to,
    value_out_to,
    losses,
    value_out_grad,
    sem,
):
    copies = [
        pltpu.make_async_copy(source, target, sem.at[i])
        for i, (source, target) in enumerate(
            (
                (grads.at[0], policy_in_to),
                (grads.at[1], value_in_to),
                (latent, latent_to),
                (policy_out_grad, policy_out_to),
                (losses, losses_to),
                (value_out_grad, value_out_to),
            )
        )
    ]
    for copy in copies[:4]:
        copy.start()
    losses[...] = misc[0, 1:2, :2] * (1.0 / total_rows)
    value_out_grad[...] = jnp.concatenate(
        [misc[i, 0:1, :] for i in range(misc.shape[0])], axis=0
    ).astype(BF16)
    for copy in copies[4:]:
        copy.start()
    for copy in copies:
        copy.wait()


def per_device(
    latent,
    actions,
    action_table,
    norm1_gain,
    w_query,
    w_key,
    w_value,
    w_out,
    key_cache,
    value_cache,
    norm2_gain,
    policy_in,
    value_in,
    policy_out,
    value_out,
    targets,
    returns,
):
    rows, width = latent.shape
    scenes = key_cache.shape[0]
    branch = rows // scenes
    heads_width = policy_in.shape[1]
    features = w_query.shape[1]
    share = branch // NARROW
    block = heads_width // Y
    half = heads_width // X
    total_rows = rows * X * Z
    vmem = pltpu.VMEM
    operands = (
        latent.reshape(scenes, branch, width),
        actions.reshape(scenes, branch),
        action_table,
        norm1_gain.reshape(1, width),
        w_query,
        w_key,
        w_value,
        w_out,
        key_cache,
        value_cache,
        norm2_gain.reshape(1, width),
        policy_in,
        value_in,
        policy_out,
        value_out.reshape(Y, 128),
        targets.reshape(scenes, branch),
        returns.reshape(scenes, branch),
    )
    operands = [pltpu.with_memory_space_constraint(operand, pltpu.HBM) for operand in operands]
    scratch = [
        vmem((scenes, branch, width), BF16),
        vmem((scenes, branch), jnp.int32),
        vmem(action_table.shape, BF16),
        vmem((1, width), F32),
        vmem((3,) + w_query.shape, BF16),
        vmem(w_out.shape, BF16),
        vmem(key_cache.shape, BF16),
        vmem(value_cache.shape, BF16),
        vmem((1, width), F32),
        vmem((2,) + policy_in.shape, BF16),
        vmem(policy_out.shape, BF16),
        vmem((Y, 128), BF16),
        vmem((scenes, branch), jnp.int32),
        vmem((scenes, branch), F32),
        vmem((NARROW, scenes, branch, width), BF16),
        vmem((NARROW, 8, branch), F32),
        vmem((scenes, branch, width), F32),
        vmem((scenes, 3, branch, features), F32),
        vmem((NARROW, scenes, branch, features), BF16),
        vmem((X, scenes, width, branch), BF16),
        vmem((scenes, branch, 2 * heads_width + 128), BF16),
        vmem((scenes, NARROW, share, 2 * heads_width + 128), BF16),
        vmem((scenes, branch, policy_out.shape[1]), F32),
        vmem((scenes, branch, 128), F32),
        vmem((2, X, scenes, share, half), BF16),
        vmem((2, X, scenes, branch, half), BF16),
        vmem((NARROW, scenes * share, block + 128), BF16),
        vmem((NARROW, scenes * share, block + 128), BF16),
        vmem((Y, 8, 128), F32),
        vmem((NARROW, 8, 128), F32),
        vmem((2, width, half), F32),
        vmem((2, width, half), BF16),
        vmem((2, Z - 1, width // Z, half), BF16),
        vmem((block, 128), F32),
        vmem((block, 128), BF16),
        vmem((X - 1, block // X, 128), BF16),
        vmem((block // X, 128), BF16),
        vmem((Z - 1, block // X, 128), BF16),
        vmem((X, 8, 128), F32),
        vmem((Z, 8, 128), F32),
        pltpu.SemaphoreType.DMA((LOADS,)),
        pltpu.SemaphoreType.DMA((SENDS,)),
        pltpu.SemaphoreType.DMA((ARRIVALS,)),
    ]
    results = pl.pallas_call(
        kernel,
        name="imagine",
        out_shape=(
            vmem((scenes, branch, width), BF16),
            vmem((2, width, heads_width), BF16),
            vmem(policy_out.shape, BF16),
            vmem((Y, 8, 128), F32),
        ),
        in_specs=[pl.BlockSpec(memory_space=pltpu.HBM)] * len(operands),
        out_specs=[pl.BlockSpec(memory_space=pltpu.VMEM)] * 4,
        scratch_shapes=scratch,
        compiler_params=pltpu.CompilerParams(
            collective_id=0, has_side_effects=True, vmem_limit_bytes=40 * 2**20
        ),
    )(*operands)
    new_latent, policy_in_grad, value_in_grad, policy_out_grad, losses, value_out_grad = pl.pallas_call(
        functools.partial(deliver, total_rows),
        name="deliver",
        out_shape=(
            jax.ShapeDtypeStruct((scenes, branch, width), BF16),
            jax.ShapeDtypeStruct(policy_in.shape, BF16),
            jax.ShapeDtypeStruct(value_in.shape, BF16),
            jax.ShapeDtypeStruct(policy_out.shape, BF16),
            jax.ShapeDtypeStruct((1, 2), F32),
            jax.ShapeDtypeStruct((Y, 128), BF16),
        ),
        in_specs=[pl.BlockSpec(memory_space=pltpu.VMEM)] * 4,
        out_specs=[pl.BlockSpec(memory_space=pltpu.HBM)] * 6,
        scratch_shapes=[
            vmem((1, 2), F32),
            vmem((Y, 128), BF16),
            pltpu.SemaphoreType.DMA((6,)),
        ],
        compiler_params=pltpu.CompilerParams(vmem_limit_bytes=8 * 2**20),
    )(*[pltpu.with_memory_space_constraint(result, pltpu.VMEM) for result in results])
    return (
        new_latent.reshape(rows, width),
        losses.reshape(2),
        policy_in_grad,
        value_in_grad,
        policy_out_grad,
        value_out_grad.reshape(heads_width),
    )


def solution(mesh):
    placed = (
        P("wide", "narrow"),
        P("wide"),
        P(None, "narrow"),
        P("narrow"),
        P(None, "narrow"),
        P(None, "narrow"),
        P(None, "narrow"),
        P(None, "narrow"),
        P("wide", None, "narrow"),
        P("wide", None, "narrow"),
        P("narrow"),
        P("narrow", None),
        P("narrow", None),
        P(),
        P(),
        P("wide"),
        P("wide"),
    )
    return jax.shard_map(
        per_device,
        mesh=mesh,
        in_specs=placed,
        out_specs=(P("wide", "narrow"), P(), P("narrow", None), P("narrow", None), P(), P()),
        check_vma=False,
    )
```

```python
import functools

import jax
import jax.numpy as jnp
from jax import lax
from jax.experimental import pallas as pl
from jax.experimental.pallas import tpu as pltpu
from jax.sharding import PartitionSpec as P

HD = 128
EPSILON = 1e-05
X, Y, Z = 4, 4, 8
NARROW = 2 * Y
MESH = pl.DeviceIdType.MESH
F32, BF16 = jnp.float32, jnp.bfloat16
LOADS, SENDS, ARRIVALS = 14, 24, 81


def nt_dot(left, right):
    return lax.dot_general(left, right, (((1,), (1,)), ((), ())), preferred_element_type=F32)


def dot(left, right):
    return jnp.dot(left, right, preferred_element_type=F32)


def kernel(
    latent_in,
    actions_in,
    table_in,
    gain1_in,
    w_query_in,
    w_key_in,
    w_value_in,
    w_out_in,
    keys_in,
    values_in,
    gain2_in,
    policy_in_in,
    value_in_in,
    policy_out_in,
    value_out_in,
    targets_in,
    returns_in,
    latent_out,
    grads_out,
    policy_out_grad,
    misc_out,
    latent,
    actions,
    table,
    gain1,
    w_qkv,
    w_out,
    keys,
    values,
    gain2,
    heads_w,
    policy_out,
    value_out,
    targets,
    returns,
    normed,
    squares,
    tokens,
    qkv,
    attended,
    gained_t,
    pre_send,
    pre_recv,
    onehot,
    returns_col,
    dpre_send,
    dpre_recv,
    factor_send,
    factor_recv,
    misc_send,
    misc_recv,
    grad_f32,
    grad_send,
    grad_recv,
    block_f32,
    block_send,
    block_recv,
    block_mid,
    block_recv_z,
    misc_x,
    misc_z,
    load_sem,
    send_sem,
    recv_sem,
):
    wide, narrow = lax.axis_index("wide"), lax.axis_index("narrow")
    x, z = wide // Z, lax.rem(wide, Z)
    y, c = narrow // 2, lax.rem(narrow, 2)
    _, scenes, branch, width = normed.shape
    total_rows = scenes * branch * X * Z
    full_width = width * NARROW

    def device(dx=0, dy=0, dz=0, dc=0):
        return (
            lax.rem(x + dx, X) * Z + lax.rem(z + dz, Z),
            lax.rem(y + dy, Y) * 2 + lax.rem(c + dc, 2),
        )

    def span(index, size):
        return pl.ds(pl.multiple_of(index * size, size), size)

    plane = [(dx, dy, dc) for dx in (2, 1, 3, 0) for dy in (2, 1, 3, 0) for dc in (1, 0)]
    plane = [o for o in plane if o != (0, 0, 0)]
    line = [(dy, dc) for dx, dy, dc in plane if dx == 0]
    z_steps = (4, 3, 5, 2, 6, 1, 7)
    x_steps = (2, 1, 3)
    y_steps = (1, 3, 2)
    barrier = pltpu.get_barrier_semaphore()
    partners = [device(dx, dy, 0, dc) for dx, dy, dc in plane] + [device(dz=d) for d in z_steps]
    for partner in partners:
        pl.semaphore_signal(barrier, inc=1, device_id=partner, device_id_type=MESH)

    places = [narrow, y * 2 + 1 - c]
    places += [lax.rem(y - d + Y, Y) * 2 + c for d in y_steps]
    places += [lax.rem(y - d + Y, Y) * 2 + 1 - c for d in y_steps]

    loads = {}

    def load(name, target, *pieces):
        sem = load_sem.at[len(loads)]
        for source, part in pieces:
            pltpu.make_async_copy(source, part, sem).start()
        loads[name] = pltpu.make_async_copy(target, target, sem)

    def ready(*names):
        for name in names:
            loads[name].wait()

    load("actions", actions, (actions_in, actions))
    load("table", table, (table_in, table))
    load("latent", latent, (latent_in, latent))
    load("gain1", gain1, (gain1_in, gain1))
    weights = (w_query_in, w_key_in, w_value_in)
    load(
        "w_qkv",
        w_qkv,
        *[
            (weights[i].at[span(place, width)], w_qkv.at[i, pl.ds(p * width, width)])
            for p, place in enumerate(places)
            for i in range(3)
        ],
    )
    load("keys", keys, (keys_in, keys))
    load("values", values, (values_in, values))
    depth = w_qkv.shape[2]
    load(
        "w_out",
        w_out,
        *[
            (w_out_in.at[span(place, depth)], w_out.at[pl.ds(p * depth, depth)])
            for p, place in enumerate(places)
        ],
    )
    load("gain2", gain2, (gain2_in, gain2))
    load("heads_w", heads_w, (policy_in_in, heads_w.at[0]), (value_in_in, heads_w.at[1]))
    load("policy_out", policy_out, (policy_out_in, policy_out))
    load("value_out", value_out, (value_out_in, value_out))
    load("targets", targets, (targets_in, targets))
    load("returns", returns, (returns_in, returns))

    groups, outgoing = {}, {}
    counts = [0]

    def group_sem(name):
        if name not in groups:
            groups[name] = counts[0]
            counts[0] += 1
        return recv_sem.at[groups[name]]

    def send(source, target, partner, out, into=None):
        if out not in outgoing:
            outgoing[out] = len(outgoing)
        if into is None:
            arrival = recv_sem.at[counts[0]]
            counts[0] += 1
        else:
            arrival = group_sem(into)
        copy = pltpu.make_async_remote_copy(
            src_ref=source,
            dst_ref=target,
            send_sem=send_sem.at[outgoing[out]],
            recv_sem=arrival,
            device_id=partner,
            device_id_type=MESH,
        )
        copy.start()
        return copy

    def arrive(*copies):
        for copy in copies:
            copy.wait_recv()

    def collect(name, whole):
        pltpu.make_async_copy(whole, whole, recv_sem.at[groups[name]]).wait()

    def finish(whole):
        for name, i in outgoing.items():
            pltpu.make_async_copy(whole[name], whole[name], send_sem.at[i]).wait()

    ready("actions", "table", "latent", "gain1")
    action_count = table.shape[0]
    action_ids = lax.broadcasted_iota(jnp.int32, (action_count, branch), 0)
    for s in range(scenes):
        chosen = (actions[s : s + 1, :] == action_ids).astype(F32).T.astype(BF16)
        token = latent[s].astype(F32) + dot(chosen, table[...])
        tokens[s] = token
        normed[0, s] = (token * gain1[...]).astype(BF16)
        square = token * token
        square = sum(square[:, i : i + 128] for i in range(0, width, 128))
        squares[0, s : s + 1, :] = jnp.sum(square.T, axis=0, keepdims=True)

    pl.semaphore_wait(barrier, len(partners))

    def gather_start(buffer, s, out):
        near = send(buffer.at[0, s], buffer.at[1, s], device(dc=1), out)
        far = [
            send(buffer.at[0, s], buffer.at[2 + i, s], device(dy=d), out)
            for i, d in enumerate(y_steps)
        ]
        return near, far

    def gather_pass(buffer, s, far, out):
        passed = []
        for i, copy in enumerate(far):
            arrive(copy)
            passed.append(send(buffer.at[2 + i, s], buffer.at[5 + i, s], device(dc=1), out))
        return passed

    def gathered(buffer, s, low, high):
        return jnp.concatenate([buffer[p, s] for p in range(low, high)], axis=1)

    gathers = [gather_start(normed, 0, "normed")]
    for dy, dc in line:
        send(squares.at[0], squares.at[2 * dy + dc], device(dy=dy, dc=dc), "squares", "squares")
    gathers.append(gather_start(normed, 1, "normed"))

    ready("targets", "returns")
    for s in range(scenes):
        onehot[s] = (targets[s : s + 1, :] == action_ids).astype(F32).T
        returns_col[s] = jnp.broadcast_to(returns[s : s + 1, :], (128, branch)).T

    scaling = HD ** (-0.5)
    heads_local = depth // HD
    attended_copies = []

    def project(s, low, high):
        rows = gathered(normed, s, low, high)
        for i in range(3):
            product = dot(rows, w_qkv[i, low * width : high * width, :])
            if low == 0:
                qkv[s, i] = product
            else:
                qkv[s, i] += product

    ready("w_qkv")
    for s in range(scenes):
        arrive(gathers[s][0])
        project(s, 0, 2)
    for s in range(scenes):
        passed = gather_pass(normed, s, gathers[s][1], "normed")
        project(s, 2, 5)
        arrive(*passed)
        project(s, 5, 8)
        if s == 0:
            collect("squares", squares.at[pl.ds(1, NARROW - 1)])
            ready("keys", "values")
        total = jnp.sum(squares[:, s : s + 1, :], axis=0)
        inverse = lax.rsqrt(total / full_width + EPSILON)
        inverse = jnp.broadcast_to(inverse, (128, branch)).T
        for h in range(heads_local):
            cols = slice(h * HD, (h + 1) * HD)
            query, key_new, value_new = (
                (qkv[s, i, :, cols] * inverse).astype(BF16) for i in range(3)
            )
            scores = nt_dot(query, keys[s, :, cols]) * scaling
            own_score = (
                jnp.sum(query.astype(F32) * key_new.astype(F32), axis=1, keepdims=True) * scaling
            )
            highest = jnp.maximum(jnp.max(scores, axis=1, keepdims=True), own_score)
            expd = jnp.exp(scores - highest)
            own_exp = jnp.exp(own_score - highest)
            share = 1.0 / (jnp.sum(expd, axis=1, keepdims=True) + own_exp)
            probs = (expd * share).astype(BF16)
            own_prob = (own_exp * share).astype(BF16).astype(F32)
            mixed = dot(probs, values[s, :, cols]) + own_prob * value_new.astype(F32)
            attended[0, s, :, cols] = mixed.astype(BF16)
        attended_copies.append(gather_start(attended, s, "attended"))

    ready("w_out", "gain2", "heads_w")
    heads_width = heads_w.shape[2]
    both = 2 * heads_width
    share_rows = branch // NARROW
    my_rows = span(narrow, share_rows)
    for s in range(scenes):
        near, far = attended_copies[s]

        def update(low, high):
            return dot(gathered(attended, s, low, high), w_out[low * depth : high * depth, :])

        arrive(near)
        tokens[s] += update(0, 2)
        passed = gather_pass(attended, s, far, "attended")
        tokens[s] += update(2, 5)
        arrive(*passed)
        state = tokens[s] + update(5, 8)
        gained = state * gain2[...]
        gained_b = gained.astype(BF16)
        gained_t[0, s] = gained.T.astype(BF16)
        for d in x_steps:
            send(gained_t.at[0, s], gained_t.at[d, s], device(dx=d), "gained", "gained")
        square = jnp.sum(state * state, axis=1, keepdims=True)
        high = square.astype(BF16).astype(F32)
        lane = lax.broadcasted_iota(jnp.int32, (branch, 128), 1)
        pre_send[s, :, both:] = jnp.where(lane < 64, high, square - high).astype(BF16)
        for i, cols in ((1, pl.ds(heads_width, heads_width + 128)), (0, pl.ds(0, heads_width))):
            pre_send[s, :, i * heads_width : (i + 1) * heads_width] = dot(
                gained_b, heads_w[i]
            ).astype(BF16)
            for dy, dc in line:
                partner = device(dy=dy, dc=dc)
                send(
                    pre_send.at[s, span(partner[1], share_rows), cols],
                    pre_recv.at[s, 2 * dy + dc, :, cols],
                    partner,
                    "pre",
                    ("pre", s, i),
                )
        pre_recv[s, 0] = pre_send[s, my_rows, :]
        latent_out[s] = state.astype(BF16)

    ready("policy_out", "value_out")

    def first_layer_sums(i, start, size):
        for s in range(scenes):
            collect(("pre", s, i), pre_recv.at[s, pl.ds(1, NARROW - 1), :, pl.ds(start, size)])

    first_layer_sums(1, heads_width, heads_width + 128)

    def summed(low, high):
        return jnp.concatenate(
            [
                sum(pre_recv[s, i, :, low:high].astype(F32) for i in range(NARROW))
                for s in range(scenes)
            ],
            axis=0,
        )

    square = summed(both, both + 128)
    square = square[:, 0:1] + square[:, 64:65]
    inverse = lax.rsqrt(square / full_width + EPSILON)

    def hidden_layer(low):
        pre = summed(low, low + heads_width) * inverse
        sigma = 1.0 / (1.0 + jnp.exp(-pre))
        slope = sigma * (1.0 + pre * (1.0 - sigma)) * inverse
        return (pre * sigma).astype(BF16), slope

    half = heads_width // X

    def share_dpre(i, dpre):
        for j in range(X):
            for s in range(scenes):
                dpre_send[i, j, s] = dpre[
                    s * share_rows : (s + 1) * share_rows, j * half : (j + 1) * half
                ]
        own = pltpu.make_async_copy(
            dpre_send.at[i, x], dpre_recv.at[i, c, 0, :, y], group_sem(("dpre", i))
        )
        own.start()
        for dx, dy, dc in plane:
            if dc == 0:
                send(
                    dpre_send.at[i, lax.rem(x + dx, X)],
                    dpre_recv.at[i, c, dx, :, y],
                    device(dx=dx, dy=dy),
                    "dpre_y" if dx == 0 else "dpre_x",
                    ("dpre", i),
                )

    factor = total_rows ** (-0.5)
    hidden, slope = hidden_layer(heads_width)
    value_hidden = hidden.astype(F32)
    value_row = value_out[...].astype(F32)
    value_row = jnp.concatenate([value_row[i : i + 1] for i in range(Y)], axis=1)
    value = jnp.sum(value_hidden * value_row, axis=1, keepdims=True)
    wanted = jnp.concatenate([returns_col[s, my_rows, :] for s in range(scenes)], axis=0)
    errors = value - wanted[:, 0:1]
    dvalue = (errors * factor).astype(BF16).astype(F32)
    share_dpre(0, (dvalue * value_row * slope).astype(BF16))

    first_layer_sums(0, 0, heads_width)
    policy_hidden, slope = hidden_layer(0)
    logits = dot(policy_hidden, policy_out[...])
    top = jnp.max(logits, axis=1, keepdims=True)
    log_total = top + jnp.log(jnp.sum(jnp.exp(logits - top), axis=1, keepdims=True))
    target = jnp.concatenate([onehot[s, my_rows, :] for s in range(scenes)], axis=0)
    dlogits = ((jnp.exp(logits - log_total) - target) * factor).astype(BF16)
    share_dpre(1, (nt_dot(dlogits, policy_out[...]) * slope).astype(BF16))

    block = heads_width // Y
    lanes = lax.broadcasted_iota(jnp.int32, (1, 128), 1)
    picked = jnp.sum(logits * target, axis=1, keepdims=True)
    sum_policy = jnp.sum(log_total - picked, axis=0, keepdims=True)
    sum_value = 0.5 * jnp.sum(errors * errors, axis=0, keepdims=True)
    loss_row = jnp.where(lanes == 0, sum_policy, jnp.where(lanes == 1, sum_value, 0.0))
    value_grad = jnp.sum(dvalue * value_hidden, axis=0, keepdims=True)
    for i in range(Y):
        for j in range(2):
            factor_send[2 * i + j, :, :block] = policy_hidden[:, i * block : (i + 1) * block]
            factor_send[2 * i + j, :, block:] = dlogits[:, j * 128 : (j + 1) * 128]
        misc_send[i] = jnp.concatenate(
            [value_grad[:, i * block : (i + 1) * block], loss_row, jnp.zeros((6, 128), F32)], axis=0
        )
    factor_recv[0] = factor_send[narrow]
    misc_recv[0] = misc_send[y]
    for dy, dc in line:
        partner, i = device(dy=dy, dc=dc), 2 * dy + dc
        send(factor_send.at[partner[1]], factor_recv.at[i], partner, "factor", "factor")
        send(misc_send.at[lax.rem(y + dy, Y)], misc_recv.at[i], partner, "misc", "misc")

    collect("gained", gained_t.at[pl.ds(1, X - 1)])
    state_t = jnp.concatenate(
        [gained_t[i, s] for i in range(X) for s in range(scenes)], axis=1
    )
    grad_rows = width // Z
    my_grad = span(z, grad_rows)
    for i in range(2):
        collect(("dpre", i), dpre_recv.at[i, c])
        arrive(send(dpre_recv.at[i, c], dpre_recv.at[i, c], device(dc=1), "dpre_c"))
        dpre = [
            dpre_recv[i, core, j, s, k]
            for j in range(X)
            for s in range(scenes)
            for k in range(Y)
            for core in range(2)
        ]
        grad = dot(state_t, jnp.concatenate(dpre, axis=0))
        grad_f32[i] = grad
        grad_send[i] = grad.astype(BF16)
        for d in z_steps:
            rows = span(lax.rem(z + d, Z), grad_rows)
            send(
                grad_send.at[i, rows], grad_recv.at[i, d - 1], device(dz=d), "grad", ("grad", i)
            )

    collect("factor", factor_recv.at[pl.ds(1, NARROW - 1)])
    collect("misc", misc_recv.at[pl.ds(1, NARROW - 1)])
    left = jnp.concatenate([factor_recv[i, :, :block] for i in range(NARROW)], axis=0)
    right = jnp.concatenate([factor_recv[i, :, block:] for i in range(NARROW)], axis=0)
    part = dot(left.astype(F32).T.astype(BF16), right)
    block_f32[...] = part
    block_send[...] = part.astype(BF16)
    misc_x[0] = sum(misc_recv[i] for i in range(NARROW))
    block_rows = block // X
    for d in x_steps:
        rows = span(lax.rem(x + d, X), block_rows)
        send(block_send.at[rows], block_recv.at[d - 1], device(dx=d), "block", "block")
        send(misc_x.at[0], misc_x.at[d], device(dx=d), "misc_x", "misc_x")

    def spread(i, rows, out, into=None, **step):
        place = grads_out.at[1 - i, rows, span(x, half)]
        return send(place, place, device(**step), out, into)

    def spread_x(i, rows):
        for d in x_steps:
            spread(i, rows, ("x", i), ("x", i, d), dx=d)

    first_rows = grad_rows // 4

    def over_z_first(i, place):
        if i == 0:
            return span(place, grad_rows)
        start = pl.multiple_of(place * grad_rows + first_rows, first_rows)
        return pl.ds(start, grad_rows - first_rows)

    my_first = pl.ds(pl.multiple_of(z * grad_rows, grad_rows), first_rows)

    along_z = []
    for i in range(2):
        collect(("grad", i), grad_recv.at[i])
        reduced = grad_f32[i, my_grad, :] + sum(grad_recv[i, j].astype(F32) for j in range(Z - 1))
        grads_out[1 - i, my_grad, span(x, half)] = reduced.astype(BF16)
        along_z.append({d: spread(i, over_z_first(i, z), ("z", i), dz=d) for d in z_steps})
        if i == 1:
            for d in x_steps:
                spread(i, my_first, "first_x", "first_x", dx=d)
        spread_x(i, over_z_first(i, z))
        if i == 0:
            collect("block", block_recv)
            collect("misc_x", misc_x.at[pl.ds(1, X - 1)])
            block_sum = block_f32[span(x, block_rows), :]
            block_sum = block_sum + sum(block_recv[j].astype(F32) for j in range(X - 1))
            block_mid[...] = block_sum.astype(BF16)
            misc_z[0] = sum(misc_x[j] for j in range(X))
            for d in z_steps:
                send(block_mid, block_recv_z.at[d - 1], device(dz=d), "block_z", "block_z")
                send(misc_z.at[0], misc_z.at[d], device(dz=d), "misc_z", "misc_z")

    def forward(i, *steps):
        for d in steps:
            arrive(along_z[i][d])
            spread_x(i, over_z_first(i, lax.rem(z - d + Z, Z)))

    forward(0, 1, 7, 2, 6)
    collect("first_x", grads_out.at[0, pl.ds(0, 3 * first_rows), pl.ds(0, half)])
    for d in z_steps:
        rows = grads_out.at[0, my_first]
        send(rows, rows, device(dz=d), "first_z", "first_z")
    collect("block_z", block_recv_z)
    collect("misc_z", misc_z.at[pl.ds(1, Z - 1)])
    reduced = block_sum + sum(block_recv_z[i].astype(F32) for i in range(Z - 1))
    block_cols = span(c, 128)
    place = policy_out_grad.at[span(y * X + x, block_rows), block_cols]
    place[...] = reduced.astype(BF16)
    block_copies = [send(place, place, device(dx=d), "block_x") for d in x_steps]
    misc_out[y] = sum(misc_z[i] for i in range(Z))
    misc_copies = [send(misc_out.at[y], misc_out.at[y], device(dy=d), "misc_y") for d in y_steps]
    forward(0, 3, 5, 4)
    arrive(*block_copies)
    place = policy_out_grad.at[span(y, block), block_cols]
    block_copies = [send(place, place, device(dy=dy, dc=dc), "block_y") for dy, dc in line]
    forward(1, 1, 7, 2, 6, 3, 5, 4)
    arrive(*misc_copies, *block_copies)
    for i, rows in ((0, width), (1, width // 4 * 3)):
        for d in x_steps:
            collect(("x", i, d), grads_out.at[1 - i, pl.ds(0, rows), span(lax.rem(x - d + X, X), half)])
    collect("first_z", grads_out.at[0, pl.ds(0, 7 * first_rows)])
    finish(
        {
            "normed": normed.at[pl.ds(0, 7)],
            "squares": squares.at[pl.ds(0, 7)],
            "attended": attended.at[pl.ds(0, 7)],
            "pre": pre_recv.at[:, pl.ds(0, 7)],
            "gained": gained_t.at[pl.ds(0, 3)],
            "dpre_x": dpre_recv.at[:, 0, pl.ds(0, 3)],
            "dpre_y": dpre_recv.at[:, 0, 0, :, pl.ds(0, 3)],
            "dpre_c": dpre_recv.at[:, 0],
            "factor": factor_recv.at[pl.ds(0, 7)],
            "misc": misc_recv.at[pl.ds(0, 7)],
            "grad": grad_recv,
            "block": block_recv,
            "misc_x": misc_x.at[pl.ds(0, 3)],
            ("z", 0): grads_out.at[0, pl.ds(0, 112)],
            ("z", 1): grads_out.at[0, pl.ds(0, 336), pl.ds(0, 128)],
            ("x", 0): grads_out.at[0, pl.ds(0, 384)],
            ("x", 1): grads_out.at[0, pl.ds(0, 288)],
            "first_x": grads_out.at[0, pl.ds(0, 48), pl.ds(0, 128)],
            "first_z": grads_out.at[0, pl.ds(0, 112)],
            "block_z": block_recv_z,
            "misc_z": misc_z.at[pl.ds(0, 7)],
            "block_x": policy_out_grad.at[pl.ds(0, 48)],
            "misc_y": misc_out.at[pl.ds(0, 3)],
            "block_y": policy_out_grad.at[pl.ds(0, 448)],
        }
    )


def deliver(
    total_rows,
    latent,
    grads,
    policy_out_grad,
    misc,
    latent_to,
    policy_in_to,
    value_in_to,
    policy_out_to,
    losses_to,
    value_out_to,
    losses,
    value_out_grad,
    sem,
):
    copies = [
        pltpu.make_async_copy(source, target, sem.at[i])
        for i, (source, target) in enumerate(
            (
                (grads.at[0], policy_in_to),
                (grads.at[1], value_in_to),
                (latent, latent_to),
                (policy_out_grad, policy_out_to),
                (losses, losses_to),
                (value_out_grad, value_out_to),
            )
        )
    ]
    for copy in copies[:4]:
        copy.start()
    losses[...] = misc[0, 1:2, :2] * (1.0 / total_rows)
    value_out_grad[...] = jnp.concatenate(
        [misc[i, 0:1, :] for i in range(misc.shape[0])], axis=0
    ).astype(BF16)
    for copy in copies[4:]:
        copy.start()
    for copy in copies:
        copy.wait()


def per_device(
    latent,
    actions,
    action_table,
    norm1_gain,
    w_query,
    w_key,
    w_value,
    w_out,
    key_cache,
    value_cache,
    norm2_gain,
    policy_in,
    value_in,
    policy_out,
    value_out,
    targets,
    returns,
):
    rows, width = latent.shape
    scenes = key_cache.shape[0]
    branch = rows // scenes
    heads_width = policy_in.shape[1]
    features = w_query.shape[1]
    share = branch // NARROW
    block = heads_width // Y
    half = heads_width // X
    total_rows = rows * X * Z
    vmem = pltpu.VMEM
    operands = (
        latent.reshape(scenes, branch, width),
        actions.reshape(scenes, branch),
        action_table,
        norm1_gain.reshape(1, width),
        w_query,
        w_key,
        w_value,
        w_out,
        key_cache,
        value_cache,
        norm2_gain.reshape(1, width),
        policy_in,
        value_in,
        policy_out,
        value_out.reshape(Y, 128),
        targets.reshape(scenes, branch),
        returns.reshape(scenes, branch),
    )
    operands = [pltpu.with_memory_space_constraint(operand, pltpu.HBM) for operand in operands]
    scratch = [
        vmem((scenes, branch, width), BF16),
        vmem((scenes, branch), jnp.int32),
        vmem(action_table.shape, BF16),
        vmem((1, width), F32),
        vmem((3,) + w_query.shape, BF16),
        vmem(w_out.shape, BF16),
        vmem(key_cache.shape, BF16),
        vmem(value_cache.shape, BF16),
        vmem((1, width), F32),
        vmem((2,) + policy_in.shape, BF16),
        vmem(policy_out.shape, BF16),
        vmem((Y, 128), BF16),
        vmem((scenes, branch), jnp.int32),
        vmem((scenes, branch), F32),
        vmem((NARROW, scenes, branch, width), BF16),
        vmem((NARROW, 8, branch), F32),
        vmem((scenes, branch, width), F32),
        vmem((scenes, 3, branch, features), F32),
        vmem((NARROW, scenes, branch, features), BF16),
        vmem((X, scenes, width, branch), BF16),
        vmem((scenes, branch, 2 * heads_width + 128), BF16),
        vmem((scenes, NARROW, share, 2 * heads_width + 128), BF16),
        vmem((scenes, branch, policy_out.shape[1]), F32),
        vmem((scenes, branch, 128), F32),
        vmem((2, X, scenes, share, half), BF16),
        vmem((2, 2, X, scenes, Y, share, half), BF16),
        vmem((NARROW, scenes * share, block + 128), BF16),
        vmem((NARROW, scenes * share, block + 128), BF16),
        vmem((Y, 8, 128), F32),
        vmem((NARROW, 8, 128), F32),
        vmem((2, width, half), F32),
        vmem((2, width, half), BF16),
        vmem((2, Z - 1, width // Z, half), BF16),
        vmem((block, 128), F32),
        vmem((block, 128), BF16),
        vmem((X - 1, block // X, 128), BF16),
        vmem((block // X, 128), BF16),
        vmem((Z - 1, block // X, 128), BF16),
        vmem((X, 8, 128), F32),
        vmem((Z, 8, 128), F32),
        pltpu.SemaphoreType.DMA((LOADS,)),
        pltpu.SemaphoreType.DMA((SENDS,)),
        pltpu.SemaphoreType.DMA((ARRIVALS,)),
    ]
    results = pl.pallas_call(
        kernel,
        name="imagine",
        out_shape=(
            vmem((scenes, branch, width), BF16),
            vmem((2, width, heads_width), BF16),
            vmem(policy_out.shape, BF16),
            vmem((Y, 8, 128), F32),
        ),
        in_specs=[pl.BlockSpec(memory_space=pltpu.HBM)] * len(operands),
        out_specs=[pl.BlockSpec(memory_space=pltpu.VMEM)] * 4,
        scratch_shapes=scratch,
        compiler_params=pltpu.CompilerParams(
            collective_id=0, has_side_effects=True, vmem_limit_bytes=40 * 2**20
        ),
    )(*operands)
    new_latent, policy_in_grad, value_in_grad, policy_out_grad, losses, value_out_grad = pl.pallas_call(
        functools.partial(deliver, total_rows),
        name="deliver",
        out_shape=(
            jax.ShapeDtypeStruct((scenes, branch, width), BF16),
            jax.ShapeDtypeStruct(policy_in.shape, BF16),
            jax.ShapeDtypeStruct(value_in.shape, BF16),
            jax.ShapeDtypeStruct(policy_out.shape, BF16),
            jax.ShapeDtypeStruct((1, 2), F32),
            jax.ShapeDtypeStruct((Y, 128), BF16),
        ),
        in_specs=[pl.BlockSpec(memory_space=pltpu.VMEM)] * 4,
        out_specs=[pl.BlockSpec(memory_space=pltpu.HBM)] * 6,
        scratch_shapes=[
            vmem((1, 2), F32),
            vmem((Y, 128), BF16),
            pltpu.SemaphoreType.DMA((6,)),
        ],
        compiler_params=pltpu.CompilerParams(vmem_limit_bytes=8 * 2**20),
    )(*[pltpu.with_memory_space_constraint(result, pltpu.VMEM) for result in results])
    return (
        new_latent.reshape(rows, width),
        losses.reshape(2),
        policy_in_grad,
        value_in_grad,
        policy_out_grad,
        value_out_grad.reshape(heads_width),
    )


def solution(mesh):
    placed = (
        P("wide", "narrow"),
        P("wide"),
        P(None, "narrow"),
        P("narrow"),
        P(None, "narrow"),
        P(None, "narrow"),
        P(None, "narrow"),
        P(None, "narrow"),
        P("wide", None, "narrow"),
        P("wide", None, "narrow"),
        P("narrow"),
        P("narrow", None),
        P("narrow", None),
        P(),
        P(),
        P("wide"),
        P("wide"),
    )
    return jax.shard_map(
        per_device,
        mesh=mesh,
        in_specs=placed,
        out_specs=(P("wide", "narrow"), P(), P("narrow", None), P("narrow", None), P(), P()),
        check_vma=False,
    )
```
